1024 devices in a mesh: dom: 64 (over z, core), dp: 16 (over y, x).
Axes of the slice: x: 4, y: 4, z: 32, core: 2. Of those that a mesh axis runs over, the one named last changes fastest.
Arguments:
- features: bfloat16 [65536, 256], P('dom'), may hold values from -6 to 6
- degree: int32 [65536], P('dom'), may hold values from 8 to 63
- send_rows: int32 [64, 64, 16], P('dom'), may hold values from 0 to 1023
- send_counts: int32 [64, 64], P('dom'), may hold values from 4 to 16, as said below
- edge_slots: int32 [64, 16, 8, 2, 128], P('dom', 'dp'), may hold values from -1 to 127, as said below
- tile_blocks: int32 [64, 16, 8, 2], P('dom', 'dp'), may hold values from 0 to 15
- w_in: bfloat16 [512, 256], replicated, may hold values from -0.25 to 0.25
- b_in: float32 [256], replicated, may hold values from -3 to 3
- w_out: bfloat16 [256, 256], replicated, may hold values from -0.375 to 0.375
- b_out: float32 [256], replicated, may hold values from -3 to 3
- cotangent: bfloat16 [65536, 256], P('dom'), may hold values from -6 to 6
Outputs:
- output: bfloat16 [65536, 256], P(('dom', 'dp'))
- grad_features: bfloat16 [65536, 256], P(('dom', 'dp'))
- grad_w_in: float32 [512, 256], replicated
- grad_b_in: float32 [256], replicated
- grad_w_out: float32 [256, 256], replicated
- grad_b_out: float32 [256], replicated
The draws below stay inside these ranges and needn't reach their ends.
Inputs may be any that keep to these rules, and one draw needn't show every extreme that they name: `send_counts`: every owner sends 16 rows to at least one partition, and at least one partition receives 16 rows from every owner. `edge_slots`: -1 marks a padding edge in both of its entries; in each tile the live edges come first and at least half of its 128 edges are live; the first tile of every device is full.
All inputs are finite; a program needn't handle non-finite values.
Results may differ from the reference program's by a relative error of at most 0.007.
Values may be sent and summed in bfloat16 or wider, within the bound.
No kernel may reach another device: no remote copies, remote signals or barrier semaphores. Data moves between devices by JAX's collectives and lax.ppermute only.
A program may use at most 32 MiB of HBM per device.

```python
import math
import jax
import jax.numpy as jnp
from jax import lax

D = 256
BLK = 128
V_DEV = 1024
CAP = 16
TILES = 8
NV = 65536
LOCAL = 2048
BLOCKS = 16
N_DOM = 64
N_DP = 16


def draw_send_counts(key, part):
    key = jax.random.fold_in(key, 11)
    key_base, key_peer, key_column = jax.random.split(key, 3)
    drawn_counts = jax.random.randint(key_base, (N_DOM, N_DOM), CAP // 4, CAP + 1)
    peer_pick = jax.random.randint(key_peer, (N_DOM, 1), 0, N_DOM)
    column = jax.random.randint(key_column, (), 0, N_DOM)
    columns = jnp.arange(N_DOM, dtype=jnp.int32)[None, :]
    filled = (columns == peer_pick) | (columns == column)
    return jnp.where(filled, CAP, drawn_counts).astype(jnp.int32)


def draw_edge_slots(key, part):
    key = jax.random.fold_in(key, 23)
    key_slot, key_live = jax.random.split(key)
    slot_ids = jax.random.randint(key_slot, (N_DOM, N_DP, TILES, 2, BLK), 0, BLK)
    live_count = jax.random.randint(key_live, (N_DOM, N_DP, TILES, 1, 1), BLK // 2, BLK + 1)
    live_count = live_count.at[:, :, 0].set(BLK)
    position = jnp.arange(BLK, dtype=jnp.int32)
    return jnp.where(position < live_count, slot_ids, -1).astype(jnp.int32)


def plant(array, stream_key, least, top_value):
    spot = [jax.random.randint(jax.random.fold_in(stream_key, axis), (), 0, length) for axis, length in enumerate(array.shape)]
    longest = array.shape.index(max(array.shape))
    next_to = spot[:longest] + [(spot[longest] + 1) % array.shape[longest]] + spot[longest + 1:]
    return array.at[tuple(spot)].set(least).at[tuple(next_to)].set(top_value)


def level_of(stream_key, dims, pieces, smallest, largest):
    loudness = 1.0
    for dim, shards_of in pieces:
        steps = jax.random.uniform(jax.random.fold_in(jax.random.fold_in(stream_key, 6), dim), (shards_of,), jnp.float32, smallest / len(pieces), largest / len(pieces))
        loudness = loudness * jnp.repeat(jnp.exp(steps), dims[dim] // shards_of).reshape((-1,) + (1,) * (len(dims) - 1 - dim))
    return loudness


def normal_values(rng, shape, width, limit, pieces=(), kind=jnp.bfloat16):
    array = jax.random.normal(rng, shape, jnp.float32) * width
    if len(pieces) > 0:
        array = level_of(rng, shape, pieces, -0.22, 0.18) * array
    return jnp.clip(array, min=-limit, max=limit).astype(kind)


def setup_inputs(seed: int = 0) -> dict:
    key_list = jax.random.split(jax.random.key(seed), 12)
    return {
        "features": normal_values(key_list[0], (NV, D), 1.0, 6.0, ((0, 64),)),
        "degree": plant(jax.random.randint(key_list[1], (NV,), 8, 64), jax.random.fold_in(key_list[1], 1), 8, 63).astype(jnp.int32),
        "send_rows": plant(jax.random.randint(key_list[2], (N_DOM, N_DOM, CAP), 0, V_DEV), jax.random.fold_in(key_list[2], 1), 0, V_DEV - 1).astype(jnp.int32),
        "send_counts": draw_send_counts(jax.random.fold_in(key_list[11], 71), 0),
        "edge_slots": draw_edge_slots(jax.random.fold_in(key_list[11], 71), 0),
        "tile_blocks": plant(jax.random.randint(key_list[5], (N_DOM, N_DP, TILES, 2), 0, BLOCKS), jax.random.fold_in(key_list[5], 1), 0, BLOCKS - 1).astype(jnp.int32),
        "w_in": normal_values(key_list[6], (2 * D, D), (2 * D) ** -0.5, 0.25),
        "b_in": normal_values(key_list[7], (D,), 0.5, 3.0, (), jnp.float32),
        "w_out": normal_values(key_list[8], (D, D), D ** -0.5, 0.375),
        "b_out": normal_values(key_list[9], (D,), 0.5, 3.0, (), jnp.float32),
        "cotangent": normal_values(key_list[10], (NV, D), 1.0, 6.0, ((0, 64),)),
    }


def silu_slope(pre_act):
    sigmoid_pre = jax.nn.sigmoid(pre_act)
    return sigmoid_pre * (1.0 + pre_act * (1.0 - sigmoid_pre))

def edge_pass(full_rows, send_rows, send_counts, edge_slots, tile_blocks, transpose):
    usable_all = jnp.arange(CAP, dtype=jnp.int32)[None, None, :] < send_counts[:, :, None]
    owners = jnp.arange(N_DOM, dtype=jnp.int32)[:, None, None] * V_DEV + send_rows

    def one_replica(gathered_sum, replica):

        def one_partition(gathered_sum, partition):
            row_ids = lax.dynamic_index_in_dim(owners, partition, 1, keepdims=False).reshape(-1)
            usable = lax.dynamic_index_in_dim(usable_all, partition, 1, keepdims=False).reshape(-1)
            mirror = jnp.where(usable[:, None], full_rows[row_ids], jnp.zeros((), full_rows.dtype))
            owned_rows = lax.dynamic_slice_in_dim(full_rows, partition * V_DEV, V_DEV, 0)
            local_table = jnp.concatenate([owned_rows, mirror], 0)
            slot_ids = edge_slots[partition, replica]
            blocks = tile_blocks[partition, replica]
            sources = (blocks[:, 0, None] * BLK + slot_ids[:, 0, :]).reshape(-1)
            targets = (blocks[:, 1, None] * BLK + slot_ids[:, 1, :]).reshape(-1)
            is_live = (slot_ids[:, 0, :] >= 0).reshape(-1)
            if transpose:
                sources, targets = (targets, sources)
            values = jnp.where(is_live[:, None], local_table[jnp.where(is_live, sources, 0)].astype(jnp.float32), 0.0)
            partial_value = jax.ops.segment_sum(values, jnp.where(is_live, targets, 0), num_segments=LOCAL)
            partial_value = lax.optimization_barrier(partial_value.astype(jnp.bfloat16)).astype(jnp.float32)
            mirror_part = jnp.where(usable[:, None], partial_value[V_DEV:], 0.0)
            gathered_sum = gathered_sum.at[row_ids].add(mirror_part)
            owned_sum = lax.dynamic_slice_in_dim(gathered_sum, partition * V_DEV, V_DEV, 0) + partial_value[:V_DEV]
            gathered_sum = lax.dynamic_update_slice_in_dim(gathered_sum, owned_sum, partition * V_DEV, 0)
            return (gathered_sum, None)
        gathered_sum, unused = lax.scan(one_partition, gathered_sum, jnp.arange(N_DOM, dtype=jnp.int32))
        return (gathered_sum, None)
    overall, unused = lax.scan(one_replica, jnp.zeros(full_rows.shape, jnp.float32), jnp.arange(N_DP, dtype=jnp.int32))
    return overall

def reference(features, degree, send_rows, send_counts, edge_slots, tile_blocks, w_in, b_in, w_out, b_out, cotangent):
    channels = features.shape[1]
    degrees = degree.astype(jnp.float32)[:, None]
    summed = edge_pass(features, send_rows, send_counts, edge_slots, tile_blocks, False)
    aggregate = (summed / degrees).astype(jnp.bfloat16)
    inputs = jnp.concatenate([features, aggregate], 1)
    pre_act = jnp.dot(inputs, w_in, preferred_element_type=jnp.float32) + b_in
    hidden = jax.nn.silu(pre_act).astype(jnp.bfloat16)
    output = (jnp.dot(hidden, w_out, preferred_element_type=jnp.float32) + b_out).astype(jnp.bfloat16)
    grad_hidden = jnp.dot(cotangent, w_out.T, preferred_element_type=jnp.float32)
    grad_pre = (grad_hidden * silu_slope(pre_act)).astype(jnp.bfloat16)
    norm_scale = 1.0 / math.sqrt(V_DEV * N_DOM)
    grad_w_out = jnp.dot(hidden.T, cotangent, preferred_element_type=jnp.float32) * norm_scale
    grad_b_out = lax.optimization_barrier(jnp.sum(cotangent.astype(jnp.float32), 0)) * norm_scale
    grad_w_in = jnp.dot(inputs.T, grad_pre, preferred_element_type=jnp.float32) * norm_scale
    grad_b_in = lax.optimization_barrier(jnp.sum(grad_pre.astype(jnp.float32), 0)) * norm_scale
    grad_self = jnp.dot(grad_pre, w_in[:channels].T, preferred_element_type=jnp.float32)
    spread = (jnp.dot(grad_pre, w_in[channels:].T, preferred_element_type=jnp.float32) / degrees).astype(jnp.bfloat16)
    grad_neigh = edge_pass(spread, send_rows, send_counts, edge_slots, tile_blocks, True)
    grad_features = (grad_self + grad_neigh).astype(jnp.bfloat16)
    return (output, grad_features, grad_w_in, grad_b_in, grad_w_out, grad_b_out)
```

```python
import math

import jax
import jax.numpy as jnp
from jax import lax
from jax.experimental import pallas as pl
from jax.experimental.pallas import tpu as pltpu
from jax.sharding import PartitionSpec as P

BF = jnp.bfloat16
F32 = jnp.float32
LANES = 128
UNROLL = 8


def matmul(a, b, ca=1, cb=0):
    return lax.dot_general(a, b, (((ca,), (cb,)), ((), ())), preferred_element_type=F32)


def hot(condition):
    return jnp.where(condition, 1.0, 0.0).astype(BF)


def row_choice(slots_row, first, count):
    width = slots_row.shape[1]
    rows = lax.broadcasted_iota(jnp.int32, (count, width), 0)
    return hot(rows == slots_row - first)


def peer_choice(n_peers, n_slots):
    cap = n_slots // n_peers
    peers = lax.broadcasted_iota(jnp.int32, (n_peers, n_slots), 0)
    slots = lax.broadcasted_iota(jnp.int32, (n_peers, n_slots), 1)
    return hot((slots >= peers * cap) & (slots < peers * cap + cap))


def pick(table, slots_row):
    total = None
    for first in range(0, table.shape[1], LANES):
        choice = row_choice(slots_row, first, LANES)
        part = matmul(table[:, first : first + LANES], choice)
        total = part if total is None else total + part
    return total


def scatter(values, slots_row, count):
    parts = []
    for first in range(0, count, LANES):
        choice = row_choice(slots_row, first, LANES)
        parts.append(matmul(values, choice, 1, 1))
    return jnp.concatenate(parts, 1)


def cap_lane(shape, cap):
    return lax.rem(lax.broadcasted_iota(jnp.int32, shape, 1), cap)


def to_peers(columns, n_peers):
    k, n_slots = columns.shape
    cap = n_slots // n_peers
    lane = cap_lane(columns.shape, cap)
    spread_out = jnp.concatenate(
        [jnp.where(lane == c, columns, 0.0).astype(BF) for c in range(cap)], 0
    )
    return matmul(peer_choice(n_peers, n_slots), spread_out, 1, 1).astype(BF)


def from_peers(arrived, cap):
    n_peers, width = arrived.shape
    k = width // cap
    n_slots = n_peers * cap
    wide = matmul(arrived, peer_choice(n_peers, n_slots), 0, 0)
    lane = cap_lane((k, n_slots), cap)
    total = jnp.zeros((k, n_slots), F32)
    for c in range(cap):
        total = jnp.where(lane == c, wide[c * k : c * k + k], total)
    return total


def first_kernel(features_ref, slots_ref, replica_ref, table_ref, payload_ref):
    k = table_ref.shape[0]
    rows = lax.broadcasted_iota(jnp.int32, (k, features_ref.shape[1]), 0)
    columns = lax.broadcasted_iota(jnp.int32, (k, features_ref.shape[1]), 1)
    mine = hot(columns == rows + replica_ref[0] * k)
    table = matmul(mine, features_ref[...], 1, 1).astype(BF)
    table_ref[...] = table
    payload_ref[...] = to_peers(pick(table, slots_ref[...]), payload_ref.shape[0])


def edges_kernel(
    transpose, arrived_ref, owned_ref, edges_ref, blocks_ref, payload_ref, own_ref, table, total
):
    k, v_count = owned_ref.shape
    n_peers = arrived_ref.shape[0]
    cap = arrived_ref.shape[1] // k
    own_blocks = v_count // LANES
    all_blocks = table.shape[0]
    mirrors = from_peers(arrived_ref[...], cap).astype(BF)
    owned = owned_ref[...]
    for b in range(own_blocks):
        table[b] = owned[:, b * LANES : b * LANES + LANES]
    for b in range(own_blocks, all_blocks):
        first = (b - own_blocks) * LANES
        table[b] = mirrors[:, first : first + LANES]
    total[...] = jnp.zeros_like(total)
    n_groups, group_rows, width = edges_ref.shape
    per_group = UNROLL
    positions = lax.broadcasted_iota(jnp.int32, (LANES, width), 0)
    a, b = (1, 0) if transpose else (0, 1)

    def group(g, carry):
        gathered = []
        for t in range(per_group):
            block = blocks_ref[g, 2 * t + a]
            slots = edges_ref[g, 2 * t + a : 2 * t + a + 1, :]
            gathered.append(matmul(table[block], hot(positions == slots)).astype(BF))
        placed = []
        for t in range(per_group):
            slots = edges_ref[g, 2 * t + b : 2 * t + b + 1, :]
            placed.append(matmul(gathered[t], hot(positions == slots), 1, 1))
        for t in range(per_group):
            block = blocks_ref[g, 2 * t + b]
            total[block] = total[block] + placed[t]
        return carry

    lax.fori_loop(0, n_groups, group, 0)
    for b in range(own_blocks):
        own_ref[:, b * LANES : b * LANES + LANES] = total[b]
    back = jnp.concatenate([total[b] for b in range(own_blocks, all_blocks)], 1)
    payload_ref[...] = to_peers(back, n_peers)


def aggregate_kernel(arrived_ref, own_ref, slots_ref, degree_ref, aggregate_ref, copies_ref):
    k, v_count = own_ref.shape
    cap = arrived_ref.shape[1] // k
    returned = from_peers(arrived_ref[...], cap).astype(BF)
    summed = own_ref[...] + scatter(returned, slots_ref[...], v_count)
    aggregate = (summed / degree_ref[...]).astype(BF)
    aggregate_ref[...] = aggregate
    for r in range(copies_ref.shape[0]):
        copies_ref[r] = aggregate


def dense_kernel(
    aggregate_ref, self_ref, gh_ref, w_in_ref, degree_ref, slots_ref, replica_ref,
    hidden_ref, grad_pre_ref, spread_ref, payload_ref,
):
    k = spread_ref.shape[0]
    channels = aggregate_ref.shape[0]
    w_neigh = w_in_ref[channels:, :]
    pre = self_ref[...] + matmul(w_neigh, aggregate_ref[...], 0, 0)
    sigmoid = 1.0 / (1.0 + jnp.exp(-pre))
    hidden_ref[...] = (pre * sigmoid).astype(BF)
    grad_pre = (gh_ref[...] * (sigmoid * (1.0 + pre * (1.0 - sigmoid)))).astype(BF)
    grad_pre_ref[...] = grad_pre
    first = pl.multiple_of(channels + replica_ref[0] * k, k)
    spread = matmul(w_in_ref[pl.ds(first, k), :], grad_pre)
    spread = (spread / degree_ref[...]).astype(BF)
    spread_ref[...] = spread
    payload_ref[...] = to_peers(pick(spread, slots_ref[...]), payload_ref.shape[0])


def weights_kernel(
    scale, hidden_ref, grad_pre_ref, cotangent_ref, table_ref, aggregate_ref, w_in_ref, w_out_ref,
    b_out_ref, replica_ref, output_ref, grad_self_ref, grads_ref, rows_ref,
):
    k, v_count = table_ref.shape
    channels = hidden_ref.shape[0]
    share = output_ref.shape[0]
    replica = replica_ref[0]
    per_block = LANES // share
    block = pl.multiple_of((replica // per_block) * LANES, LANES)
    half = pl.multiple_of(lax.rem(replica, per_block) * share, share)
    rows_ref[...] = matmul(hidden_ref[:, pl.ds(block, LANES)], w_out_ref[...], 0, 0)
    output_ref[...] = (rows_ref[pl.ds(half, share), :] + b_out_ref[...]).astype(BF)
    grad_pre = grad_pre_ref[...]
    self_t = matmul(w_in_ref[:channels, :], grad_pre_ref[:, pl.ds(block, LANES)])
    rows_ref[...] = self_t.T
    grad_self_ref[...] = rows_ref[pl.ds(half, share), :]
    ones = jnp.ones((k, v_count), BF)
    left = jnp.concatenate([table_ref[...], aggregate_ref[...], ones], 0)
    grads_in = matmul(left, grad_pre, 1, 1) * scale
    first = pl.multiple_of(replica * k, k)
    left_out = jnp.concatenate([hidden_ref[pl.ds(first, k), :], ones], 0)
    grads_out = matmul(left_out, cotangent_ref[...]) * scale
    grads_ref[...] = jnp.zeros_like(grads_ref)
    grads_ref[: 2 * k, :] = grads_in[: 2 * k]
    grads_ref[2 * k : 3 * k, :] = grads_out[:k]
    grads_ref[3 * k : 3 * k + 1, :] = grads_in[2 * k : 2 * k + 1]
    grads_ref[3 * k + 1 : 3 * k + 2, :] = grads_out[k : k + 1]


def back_kernel(arrived_ref, own_ref, slots_ref, copies_ref):
    k, v_count = own_ref.shape
    cap = arrived_ref.shape[1] // k
    n_dp = copies_ref.shape[0]
    share = v_count // n_dp
    returned = from_peers(arrived_ref[...], cap).astype(BF)
    summed = (own_ref[...] + scatter(returned, slots_ref[...], v_count)).astype(BF)
    for r in range(n_dp):
        first = r * share // LANES * LANES
        copies_ref[r] = summed[:, first : first + LANES]


def last_kernel(arrived_ref, grad_self_ref, replica_ref, grad_features_ref, rows_ref):
    share = grad_features_ref.shape[0]
    half = pl.multiple_of(lax.rem(replica_ref[0], LANES // share) * share, share)
    rows_ref[...] = arrived_ref[...].astype(F32).T
    grad_features_ref[...] = (rows_ref[pl.ds(half, share), :] + grad_self_ref[...]).astype(BF)


def call(kernel, outs, args, smem=(), scratch=(), flops=0, name=None):
    in_specs = [
        pl.BlockSpec(memory_space=pltpu.SMEM if i in smem else pltpu.VMEM) for i in range(len(args))
    ]
    shapes = [jax.ShapeDtypeStruct(s, d) for s, d in outs]
    size = sum(math.prod(s) * jnp.dtype(d).itemsize for s, d in outs)
    size += sum(x.size * x.dtype.itemsize for x in args)
    return pl.pallas_call(
        kernel,
        out_shape=shapes,
        in_specs=in_specs,
        out_specs=[pl.BlockSpec(memory_space=pltpu.VMEM) for _ in outs],
        scratch_shapes=list(scratch),
        compiler_params=pltpu.CompilerParams(vmem_limit_bytes=48 * 1024 * 1024),
        cost_estimate=pl.CostEstimate(flops=flops, bytes_accessed=size, transcendentals=0),
        name=name,
    )(*args)


def swap(values, axis):
    return lax.all_to_all(values, axis, split_axis=0, concat_axis=0, tiled=True)


def on_device(
    features,
    degree,
    send_rows,
    send_counts,
    edge_slots,
    tile_blocks,
    w_in,
    b_in,
    w_out,
    b_out,
    cotangent,
):
    n_dp = lax.axis_size("dp")
    n_dom = lax.axis_size("dom")
    replica = lax.axis_index("dp").astype(jnp.int32).reshape(1)
    v_count, channels = features.shape
    cap = send_rows.shape[2]
    k = channels // n_dp
    share = v_count // n_dp
    n_slots = n_dom * cap
    n_tiles, _, tile_rows = edge_slots.shape[2:]
    blocks_count = (v_count + n_slots) // LANES
    scale = 1.0 / math.sqrt(v_count * n_dom)

    usable = jnp.arange(cap, dtype=jnp.int32)[None, :] < send_counts[0][:, None]
    slots_row = jnp.where(usable, send_rows[0], -1).reshape(1, n_slots)
    degree_row = degree.astype(F32).reshape(1, v_count)

    table, payload = call(
        first_kernel,
        [((k, v_count), BF), ((n_dom, channels), BF)],
        [features, slots_row, replica],
        smem=(2,),
        name="first",
    )
    edge_rows = edge_slots[0, 0].reshape(2 * n_tiles, tile_rows)
    block_row = jnp.pad(tile_blocks[0, 0].reshape(1, 2 * n_tiles), ((0, 7), (0, tile_rows - 2 * n_tiles)))
    edge_rows = jnp.concatenate([edge_rows, block_row], 0)
    edges = swap(jnp.broadcast_to(edge_rows[None], (n_dp, *edge_rows.shape)), "dp")
    blocks = edges[:, 2 * n_tiles, : 2 * n_tiles]
    arrived = swap(payload, "dom")

    w_self = w_in[:channels]
    self_t = jnp.einsum("ah,va->hv", w_self, features, preferred_element_type=F32) + b_in[:, None]
    gh_t = jnp.einsum("ho,vo->hv", w_out, cotangent, preferred_element_type=F32)

    def edge_pass(arrived, owned, transpose):
        return call(
            lambda *refs: edges_kernel(transpose, *refs),
            [((n_dom, channels), BF), ((k, v_count), F32)],
            [arrived, owned, edges, blocks],
            smem=(3,),
            scratch=[
                pltpu.VMEM((blocks_count, k, LANES), BF),
                pltpu.VMEM((blocks_count, k, LANES), F32),
            ],
            name="edges_back" if transpose else "edges",
        )

    payload, own = edge_pass(arrived, table, False)
    arrived = swap(payload, "dom")
    aggregate, copies = call(
        aggregate_kernel,
        [((k, v_count), BF), ((n_dp, k, v_count), BF)],
        [arrived, own, slots_row, degree_row],
        name="aggregate",
    )
    aggregate_all = swap(copies, "dp").reshape(channels, v_count)

    hidden, grad_pre, spread, payload = call(
        dense_kernel,
        [((channels, v_count), BF), ((channels, v_count), BF), ((k, v_count), BF), ((n_dom, channels), BF)],
        [aggregate_all, self_t, gh_t, w_in, degree_row, slots_row, replica],
        smem=(6,),
        name="dense",
    )
    arrived = swap(payload, "dom")
    output, grad_self, grads = call(
        lambda *refs: weights_kernel(scale, *refs),
        [((share, channels), BF), ((share, channels), F32), ((n_dom, channels), F32)],
        [hidden, grad_pre, cotangent, table, aggregate, w_in, w_out, b_out.reshape(1, -1), replica],
        smem=(8,),
        scratch=[pltpu.VMEM((LANES, channels), F32)],
        name="weights",
    )
    payload, own = edge_pass(arrived, spread, True)
    grads = swap(grads, "dom")
    arrived = swap(payload, "dom")
    (copies,) = call(
        back_kernel,
        [((n_dp, k, LANES), BF)],
        [arrived, own, slots_row],
        name="back",
    )
    arrived = swap(copies, "dp").reshape(channels, LANES)
    (grad_features,) = call(
        last_kernel,
        [((share, channels), BF)],
        [arrived, grad_self, replica],
        smem=(2,),
        scratch=[pltpu.VMEM((LANES, channels), F32)],
        name="last",
    )
    my_row = jnp.sum(grads, 0)
    rows = swap(jnp.broadcast_to(my_row[None], (n_dom, channels)), "dom")
    used = 3 * k + 2
    rows = rows[:used]
    everything = swap(jnp.broadcast_to(rows[None], (n_dp, used, channels)), "dp")
    grad_w_in = jnp.concatenate(
        [everything[:, :k].reshape(channels, channels), everything[:, k : 2 * k].reshape(channels, channels)], 0
    )
    grad_w_out = everything[:, 2 * k : 3 * k].reshape(channels, channels)
    grad_b_in = everything[0, 3 * k]
    grad_b_out = everything[0, 3 * k + 1]
    return (output, grad_features, grad_w_in, grad_b_in, grad_w_out, grad_b_out)


def solution(mesh):
    in_specs = (
        P("dom", None),
        P("dom"),
        P("dom", None, None),
        P("dom", None),
        P("dom", "dp", None, None, None),
        P("dom", "dp", None, None),
        P(),
        P(),
        P(),
        P(),
        P("dom", None),
    )
    out_specs = (P(("dom", "dp"), None), P(("dom", "dp"), None), P(), P(), P(), P())
    return jax.shard_map(
        on_device, mesh=mesh, in_specs=in_specs, out_specs=out_specs, check_vma=False
    )
```

```python
import math

import jax
import jax.numpy as jnp
from jax import lax
from jax.experimental import pallas as pl
from jax.experimental.pallas import tpu as pltpu
from jax.sharding import PartitionSpec as P

BF = jnp.bfloat16
F32 = jnp.float32
LANES = 128
PART = 8
GROUPS = 4


def matmul(a, b, ca=1, cb=0):
    return lax.dot_general(a, b, (((ca,), (cb,)), ((), ())), preferred_element_type=F32)


def hot(condition):
    return jnp.where(condition, 1.0, 0.0).astype(BF)


def row_choice(slots_row, first, count):
    width = slots_row.shape[1]
    rows = lax.broadcasted_iota(jnp.int32, (count, width), 0)
    return hot(rows == slots_row - first)


def peer_choice(n_peers, n_slots):
    peers = lax.broadcasted_iota(jnp.int32, (n_peers, 1), 0)
    slots = lax.broadcasted_iota(jnp.int32, (1, n_slots), 1)
    return hot(slots // (n_slots // n_peers) == peers)


def pick(table, slots_row):
    total = None
    for first in range(0, table.shape[1], LANES):
        choice = row_choice(slots_row, first, LANES)
        part = matmul(table[:, first : first + LANES], choice)
        total = part if total is None else total + part
    return total


def scatter(values, slots_row, count):
    parts = []
    for first in range(0, count, LANES):
        choice = row_choice(slots_row, first, LANES)
        parts.append(matmul(values, choice, 1, 1))
    return jnp.concatenate(parts, 1)


def cap_lane(shape, cap):
    return lax.rem(lax.broadcasted_iota(jnp.int32, shape, 1), cap)


def peer_rows(n_rows, per_peer, n_slots, cap):
    rows = lax.broadcasted_iota(jnp.int32, (n_rows, 1), 0)
    part = lax.rem(rows, per_peer)
    used = jnp.where(part < cap // PART, rows // per_peer * (cap // PART) + part, -1)
    slots = lax.broadcasted_iota(jnp.int32, (1, n_slots), 1) // PART
    return hot(slots == used)


def to_peers(columns, per_peer, cap):
    k, n_slots = columns.shape
    n_rows = n_slots // cap * per_peer
    lane = cap_lane(columns.shape, PART)
    spread_out = jnp.concatenate(
        [jnp.where(lane == c, columns, 0.0).astype(BF) for c in range(PART)], 0
    )
    return matmul(peer_rows(n_rows, per_peer, n_slots, cap), spread_out, 1, 1)


def from_peers(arrived, per_peer, cap):
    n_rows, width = arrived.shape
    k = width // PART
    n_slots = n_rows // per_peer * cap
    wide = matmul(arrived, peer_rows(n_rows, per_peer, n_slots, cap), 0, 0)
    lane = cap_lane((k, n_slots), PART)
    total = jnp.zeros((k, n_slots), F32)
    for c in range(PART):
        total = jnp.where(lane == c, wide[c * k : c * k + k], total)
    return total


def slots_of(send_rows, send_counts, v_count):
    n_peers, cap = send_rows.shape
    n_slots = n_peers * cap
    chosen = peer_choice(n_peers, n_slots)
    base = 32
    high = send_rows // base
    low = send_rows - high * base
    lane = cap_lane((cap, n_slots), cap)
    c = lax.broadcasted_iota(jnp.int32, (cap, n_slots), 0)
    both = matmul(high.astype(F32).astype(BF), chosen, 0, 0) * base + matmul(
        low.astype(F32).astype(BF), chosen, 0, 0
    )
    rows = jnp.sum(jnp.where(lane == c, both, 0.0), 0, keepdims=True)
    counts = jnp.broadcast_to(send_counts.astype(F32), (8, n_peers)).astype(BF)
    counts = matmul(counts, chosen)[:1]
    unused = cap_lane((1, n_slots), cap).astype(F32) >= counts
    return jnp.where(unused, float(v_count), rows).astype(jnp.int32)


def first_kernel(
    features_ref, send_rows_ref, send_counts_ref, replica_ref, table_ref, slots_ref, payload_ref
):
    k, v_count = table_ref.shape
    rows = lax.broadcasted_iota(jnp.int32, (k, features_ref.shape[1]), 0)
    columns = lax.broadcasted_iota(jnp.int32, (k, features_ref.shape[1]), 1)
    mine = hot(columns == rows + replica_ref[0] * k)
    table = matmul(mine, features_ref[...], 1, 1).astype(BF)
    table_ref[...] = table
    slots = slots_of(send_rows_ref[...], send_counts_ref[...], v_count)
    slots_ref[...] = slots
    cap = send_rows_ref.shape[1]
    payload_ref[...] = to_peers(pick(table, slots), cap // PART, cap).astype(BF)


def edges_kernel(
    cap, per_peer, transpose, arrived_ref, owned_ref, edges_ref, blocks_ref, payload_ref, own_ref,
    table, total,
):
    k, v_count = owned_ref.shape
    own_blocks = v_count // LANES
    all_blocks = table.shape[0]
    arrived = arrived_ref[...]
    mirrors = from_peers(arrived, per_peer, cap).astype(BF)
    owned = owned_ref[...]
    for b in range(own_blocks):
        table[b] = owned[:, b * LANES : b * LANES + LANES]
    for b in range(own_blocks, all_blocks):
        first = (b - own_blocks) * LANES
        table[b] = mirrors[:, first : first + LANES]
    total[...] = jnp.zeros_like(total)
    n_groups, group_rows, width = edges_ref.shape
    per_group = (group_rows - 8) // 2
    positions = lax.broadcasted_iota(jnp.int32, (LANES, width), 0)
    a, b = (1, 0) if transpose else (0, 1)

    together = math.gcd(n_groups, GROUPS)
    tiles = [(j, t) for j in range(together) for t in range(per_group)]

    def group(i, carry):
        g = i * together
        gathered = []
        for j, t in tiles:
            block = blocks_ref[g + j, 2 * t + a]
            slots = edges_ref[g + j, 2 * t + a : 2 * t + a + 1, :]
            gathered.append(matmul(table[block], hot(positions == slots)).astype(BF))
        placed = []
        for (j, t), values in zip(tiles, gathered):
            slots = edges_ref[g + j, 2 * t + b : 2 * t + b + 1, :]
            placed.append(matmul(values, hot(positions == slots), 1, 1))
        for (j, t), values in zip(tiles, placed):
            block = blocks_ref[g + j, 2 * t + b]
            total[block] = total[block] + values
        return carry

    lax.fori_loop(0, n_groups // together, group, 0)
    for b in range(own_blocks):
        own_ref[:, b * LANES : b * LANES + LANES] = total[b]
    back = jnp.concatenate([total[b] for b in range(own_blocks, all_blocks)], 1)
    outgoing = to_peers(back, per_peer, cap)
    if per_peer > cap // PART:
        parts = per_peer - cap // PART
        rows = lax.broadcasted_iota(jnp.int32, (8, arrived.shape[0]), 1)
        part = lax.broadcasted_iota(jnp.int32, (8, arrived.shape[0]), 0)
        chosen = hot(lax.rem(rows, per_peer) == part + cap // PART)
        sums = matmul(chosen, arrived)
        place = lax.rem(lax.broadcasted_iota(jnp.int32, outgoing.shape, 0), per_peer)
        for h in range(parts):
            outgoing = jnp.where(place == cap // PART + h, sums[h : h + 1], outgoing)
    payload_ref[...] = outgoing.astype(BF)


def aggregate_kernel(cap, arrived_ref, own_ref, slots_ref, degree_ref, aggregate_ref, copies_ref):
    k, v_count = own_ref.shape
    returned = from_peers(arrived_ref[...], cap // PART, cap).astype(BF)
    summed = own_ref[...] + scatter(returned, slots_ref[...], v_count)
    aggregate = (summed / degree_ref[...]).astype(BF)
    aggregate_ref[...] = aggregate
    for r in range(copies_ref.shape[0]):
        copies_ref[r] = aggregate


def dense_kernel(
    scale, cap, aggregate_ref, self_ref, gh_ref, w_in_ref, degree_ref, slots_ref, table_ref, mine_ref,
    cotangent_ref, replica_ref, hidden_out_ref, grad_pre_out_ref, spread_ref, payload_ref, hidden_ref,
    grad_pre_ref,
):
    k, v_count = spread_ref.shape
    channels = aggregate_ref.shape[0]
    w_neigh = w_in_ref[channels:, :]
    pre = self_ref[...] + matmul(w_neigh, aggregate_ref[...], 0, 0)
    sigmoid = 1.0 / (1.0 + jnp.exp(-pre))
    hidden_ref[...] = (pre * sigmoid).astype(BF)
    grad_pre = (gh_ref[...] * (sigmoid * (1.0 + pre * (1.0 - sigmoid)))).astype(BF)
    grad_pre_ref[...] = grad_pre
    per_block = LANES // (v_count * k // channels)
    block = pl.multiple_of((replica_ref[0] // per_block) * LANES, LANES)
    hidden_out_ref[...] = hidden_ref[:, pl.ds(block, LANES)]
    grad_pre_out_ref[...] = grad_pre_ref[:, pl.ds(block, LANES)]
    first = pl.multiple_of(channels + replica_ref[0] * k, k)
    spread = matmul(w_in_ref[pl.ds(first, k), :], grad_pre)
    spread = (spread / degree_ref[...]).astype(BF)
    spread_ref[...] = spread

    ones = jnp.ones((k, v_count), BF)
    left = jnp.concatenate([table_ref[...], mine_ref[...], ones], 0)
    grads_in = (matmul(left, grad_pre, 1, 1) * scale).astype(BF)
    first = pl.multiple_of(replica_ref[0] * k, k)
    left = jnp.concatenate([hidden_ref[pl.ds(first, k), :], ones], 0)
    grads_out = (matmul(left, cotangent_ref[...]) * scale).astype(BF)
    grads = jnp.concatenate([grads_in[: 2 * k], grads_out[:k], grads_in[2 * k :], grads_out[k:]], 0)

    parts = cap // PART
    halves = channels // LANES
    per_peer = parts + halves
    payload = to_peers(pick(spread, slots_ref[...]), per_peer, cap)
    n_rows = payload.shape[0]
    rows = lax.broadcasted_iota(jnp.int32, (n_rows, grads.shape[0]), 0)
    source = lax.broadcasted_iota(jnp.int32, (n_rows, grads.shape[0]), 1)
    peer = jnp.where(source == 4 * k, 3 * k + 1, jnp.where(source > 3 * k, -1, source))
    for h in range(halves):
        chosen = hot((rows // per_peer == peer) & (lax.rem(rows, per_peer) == parts + h))
        payload = payload + matmul(chosen, grads[:, h * LANES : h * LANES + LANES])
    payload_ref[...] = payload.astype(BF)


def rows_kernel(
    hidden_ref, grad_pre_ref, w_in_ref, w_out_ref, b_out_ref, replica_ref, output_ref, grad_self_ref,
    rows_ref,
):
    channels = hidden_ref.shape[0]
    share = output_ref.shape[0]
    replica = replica_ref[0]
    per_block = LANES // share
    half = pl.multiple_of(lax.rem(replica, per_block) * share, share)
    rows_ref[...] = matmul(hidden_ref[...], w_out_ref[...], 0, 0)
    output_ref[...] = (rows_ref[pl.ds(half, share), :] + b_out_ref[...]).astype(BF)
    rows_ref[...] = matmul(w_in_ref[:channels, :], grad_pre_ref[...]).T
    grad_self_ref[...] = rows_ref[pl.ds(half, share), :]


def back_kernel(cap, per_peer, arrived_ref, own_ref, slots_ref, copies_ref):
    k, v_count = own_ref.shape
    n_dp = copies_ref.shape[0]
    share = v_count // n_dp
    arrived = arrived_ref[...]
    returned = from_peers(arrived, per_peer, cap).astype(BF)
    summed = (own_ref[...] + scatter(returned, slots_ref[...], v_count)).astype(BF)
    n_rows = copies_ref.shape[1] - k
    parts = cap // PART
    halves = per_peer - parts
    to = lax.broadcasted_iota(jnp.int32, (n_rows, arrived.shape[0]), 0)
    source = lax.broadcasted_iota(jnp.int32, (n_rows, arrived.shape[0]), 1)
    peer, half = source // per_peer, lax.rem(source, per_peer) - parts
    place = jnp.where(peer < 3 * k, half * (3 * k) + peer, halves * 3 * k + (peer - 3 * k) * halves + half)
    chosen = hot((place == to) & (half >= 0))
    grads = matmul(chosen, arrived).astype(BF)
    for r in range(n_dp):
        first = r * share // LANES * LANES
        copies_ref[r, :k] = summed[:, first : first + LANES]
        copies_ref[r, k:] = grads


def last_kernel(
    arrived_ref, grad_self_ref, replica_ref, grad_features_ref, grad_w_in_ref, grad_b_in_ref,
    grad_w_out_ref, grad_b_out_ref, rows_ref,
):
    share, channels = grad_features_ref.shape
    n_dp = arrived_ref.shape[0]
    k = channels // n_dp
    half = pl.multiple_of(lax.rem(replica_ref[0], LANES // share) * share, share)
    columns = jnp.concatenate([arrived_ref[r, :k] for r in range(n_dp)], 0)
    rows_ref[...] = columns.astype(F32).T
    grad_features_ref[...] = (rows_ref[pl.ds(half, share), :] + grad_self_ref[...]).astype(BF)
    halves = channels // LANES
    for h in range(halves):
        lanes = slice(h * LANES, h * LANES + LANES)
        first = k + h * 3 * k
        for r in range(n_dp):
            rows = slice(r * k, r * k + k)
            grad_w_in_ref[rows, lanes] = arrived_ref[r, first : first + k].astype(F32)
            second = slice(channels + r * k, channels + r * k + k)
            grad_w_in_ref[second, lanes] = arrived_ref[r, first + k : first + 2 * k].astype(F32)
            grad_w_out_ref[rows, lanes] = arrived_ref[r, first + 2 * k : first + 3 * k].astype(F32)
        biases = arrived_ref[0, k + halves * 3 * k :].astype(F32)
        grad_b_in_ref[:, lanes] = biases[h : h + 1]
        grad_b_out_ref[:, lanes] = biases[halves + h : halves + h + 1]


def call(kernel, outs, args, smem=(), scratch=(), flops=0, name=None):
    in_specs = [
        pl.BlockSpec(memory_space=pltpu.SMEM if i in smem else pltpu.VMEM) for i in range(len(args))
    ]
    shapes = [jax.ShapeDtypeStruct(s, d) for s, d in outs]
    size = sum(math.prod(s) * jnp.dtype(d).itemsize for s, d in outs)
    size += sum(x.size * x.dtype.itemsize for x in args)
    return pl.pallas_call(
        kernel,
        out_shape=shapes,
        in_specs=in_specs,
        out_specs=[pl.BlockSpec(memory_space=pltpu.VMEM) for _ in outs],
        scratch_shapes=list(scratch),
        compiler_params=pltpu.CompilerParams(vmem_limit_bytes=16 * 1024 * 1024),
        cost_estimate=pl.CostEstimate(flops=flops, bytes_accessed=size, transcendentals=0),
        name=name,
    )(*args)


def swap(values, axis):
    return lax.all_to_all(values, axis, split_axis=0, concat_axis=0, tiled=True)


def on_device(
    features,
    degree,
    send_rows,
    send_counts,
    edge_slots,
    tile_blocks,
    w_in,
    b_in,
    w_out,
    b_out,
    cotangent,
):
    n_dp = lax.axis_size("dp")
    n_dom = lax.axis_size("dom")
    replica = lax.axis_index("dp").astype(jnp.int32).reshape(1)
    v_count, channels = features.shape
    cap = send_rows.shape[2]
    k = channels // n_dp
    share = v_count // n_dp
    n_slots = n_dom * cap
    n_tiles, _, tile_rows = edge_slots.shape[2:]
    blocks_count = (v_count + n_slots) // LANES
    scale = 1.0 / math.sqrt(v_count * n_dom)

    degree_row = degree.astype(F32).reshape(1, v_count)
    parts = cap // PART
    more = parts + channels // LANES

    edges = edge_slots[0, 0].reshape(2 * n_tiles, tile_rows)
    block_row = tile_blocks[0, 0].reshape(1, 2 * n_tiles)
    edges = jnp.concatenate([edges, jnp.pad(block_row, ((0, 7), (0, tile_rows - 2 * n_tiles)))], 0)
    edges = swap(jnp.broadcast_to(edges[None], (n_dp, *edges.shape)), "dp")
    blocks = edges[:, 2 * n_tiles, : 2 * n_tiles]

    table, slots_row, payload = call(
        first_kernel,
        [((k, v_count), BF), ((1, n_slots), jnp.int32), ((n_dom * parts, LANES), BF)],
        [features, send_rows[0], send_counts, replica],
        smem=(3,),
        name="first",
    )
    arrived = swap(payload, "dom")

    w_self = w_in[:channels]
    self_t = jnp.einsum("ah,va->hv", w_self, features, preferred_element_type=F32) + b_in[:, None]
    gh_t = jnp.einsum("ho,vo->hv", w_out, cotangent, preferred_element_type=F32)

    def edge_pass(arrived, owned, per_peer, transpose):
        return call(
            lambda *refs: edges_kernel(cap, per_peer, transpose, *refs),
            [((n_dom * per_peer, LANES), BF), ((k, v_count), F32)],
            [arrived, owned, edges, blocks],
            smem=(3,),
            scratch=[
                pltpu.VMEM((blocks_count, k, LANES), BF),
                pltpu.VMEM((blocks_count, k, LANES), F32),
            ],
            name="edges_back" if transpose else "edges",
        )

    payload, own = edge_pass(arrived, table, parts, False)
    arrived = swap(payload, "dom")
    aggregate, copies = call(
        lambda *refs: aggregate_kernel(cap, *refs),
        [((k, v_count), BF), ((n_dp, k, v_count), BF)],
        [arrived, own, slots_row, degree_row],
        name="aggregate",
    )
    aggregate_all = swap(copies, "dp").reshape(channels, v_count)

    hidden, grad_pre, spread, payload = call(
        lambda *refs: dense_kernel(scale, cap, *refs),
        [((channels, LANES), BF), ((channels, LANES), BF), ((k, v_count), BF), ((n_dom * more, LANES), BF)],
        [aggregate_all, self_t, gh_t, w_in, degree_row, slots_row, table, aggregate, cotangent, replica],
        smem=(9,),
        scratch=[pltpu.VMEM((channels, v_count), BF), pltpu.VMEM((channels, v_count), BF)],
        name="dense",
    )
    arrived = swap(payload, "dom")
    output, grad_self = call(
        rows_kernel,
        [((share, channels), BF), ((share, channels), F32)],
        [hidden, grad_pre, w_in, w_out, b_out.reshape(1, -1), replica],
        smem=(5,),
        scratch=[pltpu.VMEM((LANES, channels), F32)],
        name="rows",
    )
    payload, own = edge_pass(arrived, spread, more, True)
    arrived = swap(payload, "dom")
    grad_rows = 2 * 3 * k + k
    (copies,) = call(
        lambda *refs: back_kernel(cap, more, *refs),
        [((n_dp, k + grad_rows, LANES), BF)],
        [arrived, own, slots_row],
        name="back",
    )
    arrived = swap(copies, "dp")
    grad_features, grad_w_in, grad_b_in, grad_w_out, grad_b_out = call(
        last_kernel,
        [
            ((share, channels), BF),
            ((2 * channels, channels), F32),
            ((1, channels), F32),
            ((channels, channels), F32),
            ((1, channels), F32),
        ],
        [arrived, grad_self, replica],
        smem=(2,),
        scratch=[pltpu.VMEM((LANES, channels), F32)],
        name="last",
    )
    return (output, grad_features, grad_w_in, grad_b_in[0], grad_w_out, grad_b_out[0])


def solution(mesh):
    in_specs = (
        P("dom", None),
        P("dom"),
        P("dom", None, None),
        P("dom", None),
        P("dom", "dp", None, None, None),
        P("dom", "dp", None, None),
        P(),
        P(),
        P(),
        P(),
        P("dom", None),
    )
    out_specs = (P(("dom", "dp"), None), P(("dom", "dp"), None), P(), P(), P(), P())
    return jax.shard_map(
        on_device, mesh=mesh, in_specs=in_specs, out_specs=out_specs, check_vma=False
    )
```

```python
import math

import jax
import jax.numpy as jnp
from jax import lax
from jax.experimental import pallas as pl
from jax.experimental.pallas import tpu as pltpu
from jax.sharding import PartitionSpec as P

BF = jnp.bfloat16
F32 = jnp.float32
LANES = 128
PART = 8
GROUPS = 8


def matmul(a, b, ca=1, cb=0):
    return lax.dot_general(a, b, (((ca,), (cb,)), ((), ())), preferred_element_type=F32)


def hot(condition):
    return jnp.where(condition, 1.0, 0.0).astype(BF)


def row_choice(slots_row, first, count):
    width = slots_row.shape[1]
    rows = lax.broadcasted_iota(jnp.int32, (count, width), 0)
    return hot(rows == slots_row - first)


def peer_choice(n_peers, n_slots):
    peers = lax.broadcasted_iota(jnp.int32, (n_peers, 1), 0)
    slots = lax.broadcasted_iota(jnp.int32, (1, n_slots), 1)
    return hot(slots // (n_slots // n_peers) == peers)


def pick(table, slots_row):
    total = None
    for first in range(0, table.shape[1], LANES):
        choice = row_choice(slots_row, first, LANES)
        part = matmul(table[:, first : first + LANES], choice)
        total = part if total is None else total + part
    return total


def scatter(values, slots_row, count):
    parts = []
    for first in range(0, count, LANES):
        choice = row_choice(slots_row, first, LANES)
        parts.append(matmul(values, choice, 1, 1))
    return jnp.concatenate(parts, 1)


def cap_lane(shape, cap):
    return lax.rem(lax.broadcasted_iota(jnp.int32, shape, 1), cap)


def peer_rows(n_rows, per_peer, n_slots, cap):
    rows = lax.broadcasted_iota(jnp.int32, (n_rows, 1), 0)
    part = lax.rem(rows, per_peer)
    used = jnp.where(part < cap // PART, rows // per_peer * (cap // PART) + part, -1)
    slots = lax.broadcasted_iota(jnp.int32, (1, n_slots), 1) // PART
    return hot(slots == used)


def to_peers(columns, per_peer, cap):
    k, n_slots = columns.shape
    n_rows = n_slots // cap * per_peer
    lane = cap_lane(columns.shape, PART)
    spread_out = jnp.concatenate(
        [jnp.where(lane == c, columns, 0.0).astype(BF) for c in range(PART)], 0
    )
    return matmul(peer_rows(n_rows, per_peer, n_slots, cap), spread_out, 1, 1)


def from_peers(arrived, per_peer, cap):
    n_rows, width = arrived.shape
    k = width // PART
    n_slots = n_rows // per_peer * cap
    wide = matmul(arrived, peer_rows(n_rows, per_peer, n_slots, cap), 0, 0)
    lane = cap_lane((k, n_slots), PART)
    total = jnp.zeros((k, n_slots), F32)
    for c in range(PART):
        total = jnp.where(lane == c, wide[c * k : c * k + k], total)
    return total


def slots_of(send_rows, send_counts, v_count):
    n_peers, cap = send_rows.shape
    n_slots = n_peers * cap
    chosen = peer_choice(n_peers, n_slots)
    base = 32
    high = send_rows // base
    low = send_rows - high * base
    lane = cap_lane((cap, n_slots), cap)
    c = lax.broadcasted_iota(jnp.int32, (cap, n_slots), 0)
    both = matmul(high.astype(F32).astype(BF), chosen, 0, 0) * base + matmul(
        low.astype(F32).astype(BF), chosen, 0, 0
    )
    rows = jnp.sum(jnp.where(lane == c, both, 0.0), 0, keepdims=True)
    counts = jnp.broadcast_to(send_counts.astype(F32), (8, n_peers)).astype(BF)
    counts = matmul(counts, chosen)[:1]
    unused = cap_lane((1, n_slots), cap).astype(F32) >= counts
    return jnp.where(unused, float(v_count), rows).astype(jnp.int32)


def first_kernel(
    features_ref, send_rows_ref, send_counts_ref, replica_ref, table_ref, slots_ref, payload_ref
):
    k, v_count = table_ref.shape
    rows = lax.broadcasted_iota(jnp.int32, (k, features_ref.shape[1]), 0)
    columns = lax.broadcasted_iota(jnp.int32, (k, features_ref.shape[1]), 1)
    mine = hot(columns == rows + replica_ref[0] * k)
    table = matmul(mine, features_ref[...], 1, 1).astype(BF)
    table_ref[...] = table
    slots = slots_of(send_rows_ref[...], send_counts_ref[...], v_count)
    slots_ref[...] = slots
    cap = send_rows_ref.shape[1]
    payload_ref[...] = to_peers(pick(table, slots), cap // PART, cap).astype(BF)


def edges_kernel(
    cap, per_peer, transpose, arrived_ref, owned_ref, edges_ref, blocks_ref, payload_ref, own_ref,
    table, total,
):
    k, v_count = owned_ref.shape
    own_blocks = v_count // LANES
    all_blocks = table.shape[0]
    arrived = arrived_ref[...]
    mirrors = from_peers(arrived, per_peer, cap).astype(BF)
    owned = owned_ref[...]
    for b in range(own_blocks):
        table[b] = owned[:, b * LANES : b * LANES + LANES]
    for b in range(own_blocks, all_blocks):
        first = (b - own_blocks) * LANES
        table[b] = mirrors[:, first : first + LANES]
    total[...] = jnp.zeros_like(total)
    n_groups, group_rows, width = edges_ref.shape
    per_group = group_rows // 3
    positions = lax.broadcasted_iota(jnp.int32, (LANES, 2 * width), 0)
    a, b = (1, 0) if transpose else (0, 1)
    together = math.gcd(n_groups, GROUPS)
    tiles = [(j, t) for j in range(together) for t in range(per_group)]
    pairs = list(zip(tiles[::2], tiles[1::2]))

    def halves(product):
        return product[:k, :LANES], product[k:, LANES:]

    def group(i, carry):
        g = i * together

        def slots(tile, side):
            row = 2 * tile[1] + side
            return edges_ref[g + tile[0], row : row + 1, :]

        def block(tile, side):
            return blocks_ref[g + tile[0], 2 * tile[1] + side]

        gathered = []
        for one, two in pairs:
            left = jnp.concatenate([table[block(one, a)], table[block(two, a)]], 0)
            right = hot(positions == jnp.concatenate([slots(one, a), slots(two, a)], 1))
            gathered.append(jnp.concatenate(halves(matmul(left, right)), 0).astype(BF))
        placed = []
        for (one, two), values in zip(pairs, gathered):
            rows = positions[:, :width]
            right = jnp.concatenate([hot(rows == slots(one, b)), hot(rows == slots(two, b))], 0)
            placed.extend(halves(matmul(values, right, 1, 1)))
        for tile, values in zip(tiles, placed):
            at = block(tile, b)
            total[at] = total[at] + values
        return carry

    lax.fori_loop(0, n_groups // together, group, 0)
    for b in range(own_blocks):
        own_ref[:, b * LANES : b * LANES + LANES] = total[b]
    back = jnp.concatenate([total[b] for b in range(own_blocks, all_blocks)], 1)
    outgoing = to_peers(back, per_peer, cap)
    if per_peer > cap // PART:
        parts = per_peer - cap // PART
        rows = lax.broadcasted_iota(jnp.int32, (8, arrived.shape[0]), 1)
        part = lax.broadcasted_iota(jnp.int32, (8, arrived.shape[0]), 0)
        chosen = hot(lax.rem(rows, per_peer) == part + cap // PART)
        sums = matmul(chosen, arrived)
        place = lax.rem(lax.broadcasted_iota(jnp.int32, outgoing.shape, 0), per_peer)
        for h in range(parts):
            outgoing = jnp.where(place == cap // PART + h, sums[h : h + 1], outgoing)
    payload_ref[...] = outgoing.astype(BF)


def aggregate_kernel(cap, arrived_ref, own_ref, slots_ref, degree_ref, aggregate_ref, copies_ref):
    k, v_count = own_ref.shape
    returned = from_peers(arrived_ref[...], cap // PART, cap).astype(BF)
    summed = own_ref[...] + scatter(returned, slots_ref[...], v_count)
    aggregate = (summed / degree_ref[...]).astype(BF)
    aggregate_ref[...] = aggregate
    for r in range(copies_ref.shape[0]):
        copies_ref[r] = aggregate


def dense_kernel(
    scale, cap, aggregate_ref, self_ref, gh_ref, w_neigh_ref, degree_ref, slots_ref, table_ref, mine_ref,
    cotangent_ref, replica_ref, hidden_out_ref, grad_pre_out_ref, spread_ref, payload_ref, hidden_ref,
    grad_pre_ref,
):
    k, v_count = spread_ref.shape
    channels = aggregate_ref.shape[0]
    pre = self_ref[...] + matmul(w_neigh_ref[...], aggregate_ref[...], 0, 0)
    sigmoid = 1.0 / (1.0 + jnp.exp(-pre))
    hidden_ref[...] = (pre * sigmoid).astype(BF)
    grad_pre = (gh_ref[...] * (sigmoid * (1.0 + pre * (1.0 - sigmoid)))).astype(BF)
    grad_pre_ref[...] = grad_pre
    per_block = LANES // (v_count * k // channels)
    block = pl.multiple_of((replica_ref[0] // per_block) * LANES, LANES)
    hidden_out_ref[...] = hidden_ref[:, pl.ds(block, LANES)]
    grad_pre_out_ref[...] = grad_pre_ref[:, pl.ds(block, LANES)]
    first = pl.multiple_of(replica_ref[0] * k, k)
    spread = matmul(w_neigh_ref[pl.ds(first, k), :], grad_pre)
    spread = (spread / degree_ref[...]).astype(BF)
    spread_ref[...] = spread

    ones = jnp.ones((k, v_count), BF)
    left = jnp.concatenate([table_ref[...], mine_ref[...], ones], 0)
    grads_in = (matmul(left, grad_pre, 1, 1) * scale).astype(BF)
    left = jnp.concatenate([hidden_ref[pl.ds(first, k), :], ones], 0)
    grads_out = (matmul(left, cotangent_ref[...]) * scale).astype(BF)
    grads = jnp.concatenate([grads_in[: 2 * k], grads_out[:k], grads_in[2 * k :], grads_out[k:]], 0)

    parts = cap // PART
    halves = channels // LANES
    per_peer = parts + halves
    payload = to_peers(pick(spread, slots_ref[...]), per_peer, cap)
    n_rows = payload.shape[0]
    rows = lax.broadcasted_iota(jnp.int32, (n_rows, grads.shape[0]), 0)
    source = lax.broadcasted_iota(jnp.int32, (n_rows, grads.shape[0]), 1)
    peer = jnp.where(source == 4 * k, 3 * k + 1, jnp.where(source > 3 * k, -1, source))
    for h in range(halves):
        chosen = hot((rows // per_peer == peer) & (lax.rem(rows, per_peer) == parts + h))
        payload = payload + matmul(chosen, grads[:, h * LANES : h * LANES + LANES])
    payload_ref[...] = payload.astype(BF)


def rows_kernel(
    hidden_ref, grad_pre_ref, w_self_ref, w_out_ref, b_out_ref, replica_ref, output_ref, grad_self_ref,
    rows_ref,
):
    channels = hidden_ref.shape[0]
    share = output_ref.shape[0]
    replica = replica_ref[0]
    per_block = LANES // share
    half = pl.multiple_of(lax.rem(replica, per_block) * share, share)
    rows_ref[...] = matmul(hidden_ref[...], w_out_ref[...], 0, 0)
    output_ref[...] = (rows_ref[pl.ds(half, share), :] + b_out_ref[...]).astype(BF)
    rows_ref[...] = matmul(w_self_ref[...], grad_pre_ref[...]).T
    grad_self_ref[...] = rows_ref[pl.ds(half, share), :]


def back_kernel(cap, per_peer, arrived_ref, own_ref, slots_ref, copies_ref):
    k, v_count = own_ref.shape
    n_dp = copies_ref.shape[0]
    share = v_count // n_dp
    arrived = arrived_ref[...]
    returned = from_peers(arrived, per_peer, cap).astype(BF)
    summed = (own_ref[...] + scatter(returned, slots_ref[...], v_count)).astype(BF)
    n_rows = copies_ref.shape[1] - k
    parts = cap // PART
    halves = per_peer - parts
    to = lax.broadcasted_iota(jnp.int32, (n_rows, arrived.shape[0]), 0)
    source = lax.broadcasted_iota(jnp.int32, (n_rows, arrived.shape[0]), 1)
    peer, half = source // per_peer, lax.rem(source, per_peer) - parts
    place = jnp.where(peer < 3 * k, half * (3 * k) + peer, halves * 3 * k + (peer - 3 * k) * halves + half)
    chosen = hot((place == to) & (half >= 0))
    grads = matmul(chosen, arrived).astype(BF)
    for r in range(n_dp):
        first = r * share // LANES * LANES
        copies_ref[r, :k] = summed[:, first : first + LANES]
        copies_ref[r, k:] = grads


def last_kernel(
    arrived_ref, grad_self_ref, replica_ref, grad_features_ref, grad_w_in_ref, grad_b_in_ref,
    grad_w_out_ref, grad_b_out_ref, rows_ref,
):
    share, channels = grad_features_ref.shape
    n_dp = arrived_ref.shape[0]
    k = channels // n_dp
    half = pl.multiple_of(lax.rem(replica_ref[0], LANES // share) * share, share)
    columns = jnp.concatenate([arrived_ref[r, :k] for r in range(n_dp)], 0)
    rows_ref[...] = columns.astype(F32).T
    grad_features_ref[...] = (rows_ref[pl.ds(half, share), :] + grad_self_ref[...]).astype(BF)
    halves = channels // LANES
    for h in range(halves):
        lanes = slice(h * LANES, h * LANES + LANES)
        first = k + h * 3 * k
        for r in range(n_dp):
            rows = slice(r * k, r * k + k)
            grad_w_in_ref[rows, lanes] = arrived_ref[r, first : first + k].astype(F32)
            second = slice(channels + r * k, channels + r * k + k)
            grad_w_in_ref[second, lanes] = arrived_ref[r, first + k : first + 2 * k].astype(F32)
            grad_w_out_ref[rows, lanes] = arrived_ref[r, first + 2 * k : first + 3 * k].astype(F32)
        biases = arrived_ref[0, k + halves * 3 * k :].astype(F32)
        grad_b_in_ref[:, lanes] = biases[h : h + 1]
        grad_b_out_ref[:, lanes] = biases[halves + h : halves + h + 1]


def call(kernel, outs, args, smem=(), scratch=(), flops=0, name=None):
    in_specs = [
        pl.BlockSpec(memory_space=pltpu.SMEM if i in smem else pltpu.VMEM) for i in range(len(args))
    ]
    shapes = [jax.ShapeDtypeStruct(s, d) for s, d in outs]
    size = sum(math.prod(s) * jnp.dtype(d).itemsize for s, d in outs)
    size += sum(x.size * x.dtype.itemsize for x in args)
    return pl.pallas_call(
        kernel,
        out_shape=shapes,
        in_specs=in_specs,
        out_specs=[pl.BlockSpec(memory_space=pltpu.VMEM) for _ in outs],
        scratch_shapes=list(scratch),
        compiler_params=pltpu.CompilerParams(vmem_limit_bytes=8 * 1024 * 1024),
        cost_estimate=pl.CostEstimate(flops=flops, bytes_accessed=size, transcendentals=0),
        name=name,
    )(*args)


def swap(values, axis):
    return lax.all_to_all(values, axis, split_axis=0, concat_axis=0, tiled=True)


def on_device(
    features,
    degree,
    send_rows,
    send_counts,
    edge_slots,
    tile_blocks,
    w_in,
    b_in,
    w_out,
    b_out,
    cotangent,
):
    n_dp = lax.axis_size("dp")
    n_dom = lax.axis_size("dom")
    replica = lax.axis_index("dp").astype(jnp.int32).reshape(1)
    v_count, channels = features.shape
    cap = send_rows.shape[2]
    k = channels // n_dp
    share = v_count // n_dp
    n_slots = n_dom * cap
    n_tiles, _, tile_rows = edge_slots.shape[2:]
    blocks_count = (v_count + n_slots) // LANES
    scale = 1.0 / math.sqrt(v_count * n_dom)

    degree_row = degree.astype(F32).reshape(1, v_count)
    parts = cap // PART
    more = parts + channels // LANES

    edges = edge_slots[0, 0].reshape(2 * n_tiles, tile_rows)
    edges = jnp.concatenate([edges, jnp.pad(tile_blocks[0, 0], ((0, 0), (0, tile_rows - 2)))], 0)
    edges = swap(jnp.broadcast_to(edges[None], (n_dp, *edges.shape)), "dp")
    blocks = edges[:, 2 * n_tiles :, :2].reshape(n_dp, 2 * n_tiles)

    table, slots_row, payload = call(
        first_kernel,
        [((k, v_count), BF), ((1, n_slots), jnp.int32), ((n_dom * parts, LANES), BF)],
        [features, send_rows[0], send_counts, replica],
        smem=(3,),
        name="first",
    )
    arrived = swap(payload, "dom")

    w_self = w_in[:channels]
    self_t = jnp.einsum("ah,va->hv", w_self, features, preferred_element_type=F32) + b_in[:, None]
    gh_t = jnp.einsum("ho,vo->hv", w_out, cotangent, preferred_element_type=F32)

    def edge_pass(arrived, owned, per_peer, transpose):
        return call(
            lambda *refs: edges_kernel(cap, per_peer, transpose, *refs),
            [((n_dom * per_peer, LANES), BF), ((k, v_count), F32)],
            [arrived, owned, edges, blocks],
            smem=(3,),
            scratch=[
                pltpu.VMEM((blocks_count, k, LANES), BF),
                pltpu.VMEM((blocks_count, k, LANES), F32),
            ],
            name="edges_back" if transpose else "edges",
        )

    payload, own = edge_pass(arrived, table, parts, False)
    arrived = swap(payload, "dom")
    aggregate, copies = call(
        lambda *refs: aggregate_kernel(cap, *refs),
        [((k, v_count), BF), ((n_dp, k, v_count), BF)],
        [arrived, own, slots_row, degree_row],
        name="aggregate",
    )
    aggregate_all = swap(copies, "dp").reshape(channels, v_count)

    hidden, grad_pre, spread, payload = call(
        lambda *refs: dense_kernel(scale, cap, *refs),
        [((channels, LANES), BF), ((channels, LANES), BF), ((k, v_count), BF), ((n_dom * more, LANES), BF)],
        [aggregate_all, self_t, gh_t, w_in[channels:], degree_row, slots_row, table, aggregate, cotangent, replica],
        smem=(9,),
        scratch=[pltpu.VMEM((channels, v_count), BF), pltpu.VMEM((channels, v_count), BF)],
        name="dense",
    )
    arrived = swap(payload, "dom")
    output, grad_self = call(
        rows_kernel,
        [((share, channels), BF), ((share, channels), F32)],
        [hidden, grad_pre, w_self, w_out, b_out.reshape(1, -1), replica],
        smem=(5,),
        scratch=[pltpu.VMEM((LANES, channels), F32)],
        name="rows",
    )
    payload, own = edge_pass(arrived, spread, more, True)
    arrived = swap(payload, "dom")
    grad_rows = 2 * 3 * k + k
    (copies,) = call(
        lambda *refs: back_kernel(cap, more, *refs),
        [((n_dp, k + grad_rows, LANES), BF)],
        [arrived, own, slots_row],
        name="back",
    )
    arrived = swap(copies, "dp")
    grad_features, grad_w_in, grad_b_in, grad_w_out, grad_b_out = call(
        last_kernel,
        [
            ((share, channels), BF),
            ((2 * channels, channels), F32),
            ((1, channels), F32),
            ((channels, channels), F32),
            ((1, channels), F32),
        ],
        [arrived, grad_self, replica],
        smem=(2,),
        scratch=[pltpu.VMEM((LANES, channels), F32)],
        name="last",
    )
    return (output, grad_features, grad_w_in, grad_b_in[0], grad_w_out, grad_b_out[0])


def solution(mesh):
    in_specs = (
        P("dom", None),
        P("dom"),
        P("dom", None, None),
        P("dom", None),
        P("dom", "dp", None, None, None),
        P("dom", "dp", None, None),
        P(),
        P(),
        P(),
        P(),
        P("dom", None),
    )
    out_specs = (P(("dom", "dp"), None), P(("dom", "dp"), None), P(), P(), P(), P())
    return jax.shard_map(
        on_device, mesh=mesh, in_specs=in_specs, out_specs=out_specs, check_vma=False
    )
```

```python
import math

import jax
import jax.numpy as jnp
from jax import lax
from jax.experimental import pallas as pl
from jax.experimental.pallas import tpu as pltpu
from jax.sharding import PartitionSpec as P

BF = jnp.bfloat16
F32 = jnp.float32
LANES = 128
PART = 8
GROUPS = 8


def matmul(a, b, ca=1, cb=0):
    return lax.dot_general(a, b, (((ca,), (cb,)), ((), ())), preferred_element_type=F32)


def hot(condition):
    return jnp.where(condition, 1.0, 0.0).astype(BF)


def row_choice(slots_row, first, count):
    width = slots_row.shape[1]
    rows = lax.broadcasted_iota(jnp.int32, (count, width), 0)
    return hot(rows == slots_row - first)


def pick(table, slots_row):
    total = None
    for first in range(0, table.shape[1], LANES):
        choice = row_choice(slots_row, first, LANES)
        part = matmul(table[:, first : first + LANES], choice)
        total = part if total is None else total + part
    return total


def scatter(values, slots_row, count):
    parts = []
    for first in range(0, count, LANES):
        choice = row_choice(slots_row, first, LANES)
        parts.append(matmul(values, choice, 1, 1))
    return jnp.concatenate(parts, 1)


def cap_lane(shape, cap):
    return lax.rem(lax.broadcasted_iota(jnp.int32, shape, 1), cap)


def peer_rows(n_rows, per_peer, n_slots, cap):
    rows = lax.broadcasted_iota(jnp.int32, (n_rows, 1), 0)
    part = lax.rem(rows, per_peer)
    used = jnp.where(part < cap // PART, rows // per_peer * (cap // PART) + part, -1)
    slots = lax.broadcasted_iota(jnp.int32, (1, n_slots), 1) // PART
    return hot(slots == used)


def to_peers(columns, per_peer, cap):
    k, n_slots = columns.shape
    n_rows = n_slots // cap * per_peer
    lane = cap_lane(columns.shape, PART)
    spread_out = jnp.concatenate(
        [jnp.where(lane == c, columns, 0.0).astype(BF) for c in range(PART)], 0
    )
    return matmul(peer_rows(n_rows, per_peer, n_slots, cap), spread_out, 1, 1)


def from_peers(arrived, per_peer, cap):
    n_rows, width = arrived.shape
    k = width // PART
    n_slots = n_rows // per_peer * cap
    wide = matmul(arrived, peer_rows(n_rows, per_peer, n_slots, cap), 0, 0)
    lane = cap_lane((k, n_slots), PART)
    total = jnp.zeros((k, n_slots), F32)
    for c in range(PART):
        total = jnp.where(lane == c, wide[c * k : c * k + k], total)
    return total


def to_rows(columns):
    width = columns.shape[1] // PART
    tall = jnp.concatenate([columns[:, c * width : c * width + width] for c in range(PART)], 0)
    return tall.T.astype(BF)


def from_tall(tall):
    k = tall.shape[0] // PART
    return jnp.concatenate([tall[c * k : c * k + k] for c in range(PART)], 1)


def part_rows(n_rows, per_peer, parts):
    n_parts = n_rows // per_peer * parts
    rows = lax.broadcasted_iota(jnp.int32, (n_rows, 1), 0)
    part = lax.rem(rows, per_peer)
    source = jnp.where(part < parts, rows // per_peer * parts + part, -1)
    return hot(lax.broadcasted_iota(jnp.int32, (1, n_parts), 1) == source)


def slots_of(send_rows, send_counts, v_count):
    n_peers, cap = send_rows.shape
    n_slots = n_peers * cap
    parts = cap // PART
    width = n_peers * parts
    slots = lax.broadcasted_iota(jnp.int32, (1, n_slots), 1)
    within = lax.rem(slots, width)
    place = lax.rem(within, parts) * PART + slots // width
    chosen = hot(lax.broadcasted_iota(jnp.int32, (n_peers, 1), 0) == within // parts)
    base = 32
    high = send_rows // base
    low = send_rows - high * base
    both = matmul(high.astype(F32).astype(BF), chosen, 0, 0) * base + matmul(
        low.astype(F32).astype(BF), chosen, 0, 0
    )
    c = lax.broadcasted_iota(jnp.int32, (cap, n_slots), 0)
    rows = jnp.sum(jnp.where(c == place, both, 0.0), 0, keepdims=True)
    counts = jnp.broadcast_to(send_counts.astype(F32), (8, n_peers)).astype(BF)
    counts = matmul(counts, chosen)[:1]
    return jnp.where(place.astype(F32) >= counts, float(v_count), rows).astype(jnp.int32)


def first_kernel(
    features_ref, send_rows_ref, send_counts_ref, replica_ref, table_ref, slots_ref, payload_ref
):
    k, v_count = table_ref.shape
    rows = lax.broadcasted_iota(jnp.int32, (k, features_ref.shape[1]), 0)
    columns = lax.broadcasted_iota(jnp.int32, (k, features_ref.shape[1]), 1)
    mine = hot(columns == rows + replica_ref[0] * k)
    table = matmul(mine, features_ref[...], 1, 1).astype(BF)
    table_ref[...] = table
    slots = slots_of(send_rows_ref[...], send_counts_ref[...], v_count)
    slots_ref[...] = slots
    payload_ref[...] = to_rows(pick(table, slots))


def inputs_kernel(
    features_ref, cotangent_ref, w_in_ref, b_in_ref, w_out_ref, b_out_ref, degree_ref, self_ref, gh_ref,
    vectors_ref,
):
    w_self = w_in_ref[: features_ref.shape[1], :].astype(F32).T.astype(BF)
    self_ref[...] = matmul(w_self, features_ref[...], 1, 1) + b_in_ref[...].T
    gh_ref[...] = matmul(w_out_ref[...], cotangent_ref[...], 1, 1)
    vectors_ref[...] = jnp.zeros_like(vectors_ref)
    vectors_ref[:1, :] = degree_ref[...].astype(F32)
    vectors_ref[1:2, : b_out_ref.shape[1]] = b_out_ref[...]


def edges_kernel(
    cap, per_peer, transpose, arrived_ref, owned_ref, edges_ref, blocks_ref, ready_ref, payload_ref,
    own_ref, table, total,
):
    del ready_ref
    k, v_count = owned_ref.shape
    own_blocks = v_count // LANES
    all_blocks = table.shape[0]
    arrived = arrived_ref[...]
    mirrors = from_peers(arrived, per_peer, cap).astype(BF)
    owned = owned_ref[...]
    for b in range(own_blocks):
        table[b] = owned[:, b * LANES : b * LANES + LANES]
    for b in range(own_blocks, all_blocks):
        first = (b - own_blocks) * LANES
        table[b] = mirrors[:, first : first + LANES]
    total[...] = jnp.zeros_like(total)
    n_groups, group_rows, width = edges_ref.shape
    per_group = group_rows // 3
    positions = lax.broadcasted_iota(jnp.int32, (LANES, 2 * width), 0)
    a, b = (1, 0) if transpose else (0, 1)
    together = math.gcd(n_groups, GROUPS)
    tiles = [(j, t) for j in range(together) for t in range(per_group)]
    pairs = list(zip(tiles[::2], tiles[1::2]))

    def halves(product):
        return product[:k, :LANES], product[k:, LANES:]

    def group(i, carry):
        g = i * together

        def slots(tile, side):
            row = 2 * tile[1] + side
            return edges_ref[g + tile[0], row : row + 1, :]

        def block(tile, side):
            return blocks_ref[g + tile[0], 2 * tile[1] + side]

        gathered = []
        for one, two in pairs:
            left = jnp.concatenate([table[block(one, a)], table[block(two, a)]], 0)
            right = hot(positions == jnp.concatenate([slots(one, a), slots(two, a)], 1))
            gathered.append(jnp.concatenate(halves(matmul(left, right)), 0).astype(BF))
        placed = []
        for (one, two), values in zip(pairs, gathered):
            rows = positions[:, :width]
            right = jnp.concatenate([hot(rows == slots(one, b)), hot(rows == slots(two, b))], 0)
            placed.extend(halves(matmul(values, right, 1, 1)))
        for tile, values in zip(tiles, placed):
            at = block(tile, b)
            total[at] = total[at] + values
        return carry

    lax.fori_loop(0, n_groups // together, group, 0)
    for b in range(own_blocks):
        own_ref[:, b * LANES : b * LANES + LANES] = total[b]
    back = jnp.concatenate([total[b] for b in range(own_blocks, all_blocks)], 1)
    outgoing = to_peers(back, per_peer, cap)
    if per_peer > cap // PART:
        parts = per_peer - cap // PART
        rows = lax.broadcasted_iota(jnp.int32, (8, arrived.shape[0]), 1)
        part = lax.broadcasted_iota(jnp.int32, (8, arrived.shape[0]), 0)
        chosen = hot(lax.rem(rows, per_peer) == part + cap // PART)
        sums = matmul(chosen, arrived)
        place = lax.rem(lax.broadcasted_iota(jnp.int32, outgoing.shape, 0), per_peer)
        for h in range(parts):
            outgoing = jnp.where(place == cap // PART + h, sums[h : h + 1], outgoing)
    payload_ref[...] = outgoing.astype(BF)


def aggregate_kernel(arrived_ref, own_ref, slots_ref, vectors_ref, aggregate_ref, copies_ref):
    k, v_count = own_ref.shape
    returned = from_tall(arrived_ref[...].astype(F32).T.astype(BF))
    summed = own_ref[...] + scatter(returned, slots_ref[...], v_count)
    aggregate = (summed / vectors_ref[:1, :]).astype(BF)
    aggregate_ref[...] = aggregate
    for r in range(copies_ref.shape[0]):
        copies_ref[r] = aggregate


def dense_kernel(
    scale, cap, aggregate_ref, self_ref, gh_ref, w_in_ref, vectors_ref, slots_ref, table_ref, mine_ref,
    cotangent_ref, w_out_ref, replica_ref, output_ref, grad_self_ref, spread_ref, payload_ref,
    hidden_ref, grad_pre_ref, rows_ref,
):
    k, v_count = spread_ref.shape
    channels = aggregate_ref.shape[0]
    pre = self_ref[...] + matmul(w_in_ref[channels:, :], aggregate_ref[...], 0, 0)
    sigmoid = 1.0 / (1.0 + jnp.exp(-pre))
    hidden_ref[...] = (pre * sigmoid).astype(BF)
    grad_pre = (gh_ref[...] * (sigmoid * (1.0 + pre * (1.0 - sigmoid)))).astype(BF)
    grad_pre_ref[...] = grad_pre
    share = output_ref.shape[0]
    per_block = LANES // share
    block = pl.multiple_of((replica_ref[0] // per_block) * LANES, LANES)
    half = pl.multiple_of(lax.rem(replica_ref[0], per_block) * share, share)
    rows_ref[0] = matmul(hidden_ref[:, pl.ds(block, LANES)], w_out_ref[...], 0, 0)
    output_ref[...] = (rows_ref[0, pl.ds(half, share), :] + vectors_ref[1:2, :channels]).astype(BF)
    rows_ref[1] = matmul(w_in_ref[:channels, :], grad_pre_ref[:, pl.ds(block, LANES)]).T
    grad_self_ref[...] = rows_ref[1, pl.ds(half, share), :]
    first = pl.multiple_of(replica_ref[0] * k, k)
    spread = matmul(w_in_ref[pl.ds(pl.multiple_of(channels + first, k), k), :], grad_pre)
    spread = (spread / vectors_ref[:1, :]).astype(BF)
    spread_ref[...] = spread

    ones = jnp.ones((k, v_count), BF)
    left = jnp.concatenate([table_ref[...], mine_ref[...], ones], 0)
    grads_in = (matmul(left, grad_pre, 1, 1) * scale).astype(BF)
    left = jnp.concatenate([hidden_ref[pl.ds(first, k), :], ones], 0)
    grads_out = (matmul(left, cotangent_ref[...]) * scale).astype(BF)
    grads = jnp.concatenate([grads_in[: 2 * k], grads_out[:k], grads_in[2 * k :], grads_out[k:]], 0)

    parts = cap // PART
    halves = channels // LANES
    per_peer = parts + halves
    picked = to_rows(pick(spread, slots_ref[...]))
    n_rows = picked.shape[0] // parts * per_peer
    payload = matmul(part_rows(n_rows, per_peer, parts), picked)
    rows = lax.broadcasted_iota(jnp.int32, (n_rows, grads.shape[0]), 0)
    source = lax.broadcasted_iota(jnp.int32, (n_rows, grads.shape[0]), 1)
    peer = jnp.where(source == 4 * k, 3 * k + 1, jnp.where(source > 3 * k, -1, source))
    for h in range(halves):
        chosen = hot((rows // per_peer == peer) & (lax.rem(rows, per_peer) == parts + h))
        payload = payload + matmul(chosen, grads[:, h * LANES : h * LANES + LANES])
    payload_ref[...] = payload.astype(BF)


def back_kernel(cap, per_peer, arrived_ref, own_ref, slots_ref, copies_ref):
    k, v_count = own_ref.shape
    n_dp = copies_ref.shape[0]
    share = v_count // n_dp
    arrived = arrived_ref[...]
    tall = matmul(arrived, part_rows(arrived.shape[0], per_peer, cap // PART), 0, 0)
    returned = from_tall(tall.astype(BF))
    summed = (own_ref[...] + scatter(returned, slots_ref[...], v_count)).astype(BF)
    n_rows = copies_ref.shape[1] - k
    parts = cap // PART
    halves = per_peer - parts
    to = lax.broadcasted_iota(jnp.int32, (n_rows, arrived.shape[0]), 0)
    source = lax.broadcasted_iota(jnp.int32, (n_rows, arrived.shape[0]), 1)
    peer, half = source // per_peer, lax.rem(source, per_peer) - parts
    place = jnp.where(peer < 3 * k, half * (3 * k) + peer, halves * 3 * k + (peer - 3 * k) * halves + half)
    chosen = hot((place == to) & (half >= 0))
    grads = matmul(chosen, arrived).astype(BF)
    for r in range(n_dp):
        first = r * share // LANES * LANES
        copies_ref[r, :k] = summed[:, first : first + LANES]
        copies_ref[r, k:] = grads


def last_kernel(
    arrived_ref, grad_self_ref, rows_out_ref, replica_ref, output_ref, grad_features_ref, grad_w_in_ref,
    grad_b_in_ref, grad_w_out_ref, grad_b_out_ref, rows_ref,
):
    output_ref[...] = rows_out_ref[...]
    share, channels = grad_features_ref.shape
    n_dp = arrived_ref.shape[0]
    k = channels // n_dp
    half = pl.multiple_of(lax.rem(replica_ref[0], LANES // share) * share, share)
    columns = jnp.concatenate([arrived_ref[r, :k] for r in range(n_dp)], 0)
    rows_ref[...] = columns.astype(F32).T
    grad_features_ref[...] = (rows_ref[pl.ds(half, share), :] + grad_self_ref[...]).astype(BF)
    halves = channels // LANES
    for h in range(halves):
        lanes = slice(h * LANES, h * LANES + LANES)
        first = k + h * 3 * k
        for r in range(n_dp):
            rows = slice(r * k, r * k + k)
            grad_w_in_ref[rows, lanes] = arrived_ref[r, first : first + k].astype(F32)
            second = slice(channels + r * k, channels + r * k + k)
            grad_w_in_ref[second, lanes] = arrived_ref[r, first + k : first + 2 * k].astype(F32)
            grad_w_out_ref[rows, lanes] = arrived_ref[r, first + 2 * k : first + 3 * k].astype(F32)
        biases = arrived_ref[0, k + halves * 3 * k :].astype(F32)
        grad_b_in_ref[:, lanes] = biases[h : h + 1]
        grad_b_out_ref[:, lanes] = biases[halves + h : halves + h + 1]


def call(kernel, outs, args, smem=(), scratch=(), flops=0, name=None):
    in_specs = [
        pl.BlockSpec(memory_space=pltpu.SMEM if i in smem else pltpu.VMEM) for i in range(len(args))
    ]
    shapes = [jax.ShapeDtypeStruct(s, d) for s, d in outs]
    size = sum(math.prod(s) * jnp.dtype(d).itemsize for s, d in outs)
    size += sum(x.size * x.dtype.itemsize for x in args)
    return pl.pallas_call(
        kernel,
        out_shape=shapes,
        in_specs=in_specs,
        out_specs=[pl.BlockSpec(memory_space=pltpu.VMEM) for _ in outs],
        scratch_shapes=list(scratch),
        compiler_params=pltpu.CompilerParams(vmem_limit_bytes=8 * 1024 * 1024),
        cost_estimate=pl.CostEstimate(flops=flops, bytes_accessed=size, transcendentals=0),
        name=name,
    )(*args)


def swap(values, axis):
    return lax.all_to_all(values, axis, split_axis=0, concat_axis=0, tiled=True)


def on_device(
    features,
    degree,
    send_rows,
    send_counts,
    edge_slots,
    tile_blocks,
    w_in,
    b_in,
    w_out,
    b_out,
    cotangent,
):
    n_dp = lax.axis_size("dp")
    n_dom = lax.axis_size("dom")
    replica = lax.axis_index("dp").astype(jnp.int32).reshape(1)
    v_count, channels = features.shape
    cap = send_rows.shape[2]
    k = channels // n_dp
    share = v_count // n_dp
    n_slots = n_dom * cap
    n_tiles, _, tile_rows = edge_slots.shape[2:]
    blocks_count = (v_count + n_slots) // LANES
    scale = 1.0 / math.sqrt(v_count * n_dom)

    parts = cap // PART
    more = parts + channels // LANES

    edges = edge_slots[0, 0].reshape(2 * n_tiles, tile_rows)
    edges = jnp.concatenate([edges, jnp.pad(tile_blocks[0, 0], ((0, 0), (0, tile_rows - 2)))], 0)
    edges = swap(jnp.broadcast_to(edges[None], (n_dp, *edges.shape)), "dp")
    blocks = edges[:, 2 * n_tiles :, :2].reshape(n_dp, 2 * n_tiles)

    table, slots_row, payload = call(
        first_kernel,
        [((k, v_count), BF), ((1, n_slots), jnp.int32), ((n_dom * parts, LANES), BF)],
        [features, send_rows[0], send_counts, replica],
        smem=(3,),
        name="first",
    )
    arrived = swap(payload, "dom")
    self_t, gh_t, vectors = call(
        inputs_kernel,
        [((channels, v_count), F32), ((channels, v_count), F32), ((8, v_count), F32)],
        [
            features, cotangent, w_in, b_in.reshape(1, -1), w_out, b_out.reshape(1, -1),
            degree.reshape(1, v_count),
        ],
        name="inputs",
    )

    def edge_pass(arrived, owned, per_peer, transpose):
        return call(
            lambda *refs: edges_kernel(cap, per_peer, transpose, *refs),
            [((n_dom * per_peer, LANES), BF), ((k, v_count), F32)],
            [arrived, owned, edges, blocks, vectors],
            smem=(3,),
            scratch=[
                pltpu.VMEM((blocks_count, k, LANES), BF),
                pltpu.VMEM((blocks_count, k, LANES), F32),
            ],
            name="edges_back" if transpose else "edges",
        )

    payload, own = edge_pass(arrived, table, parts, False)
    arrived = swap(payload, "dom")
    aggregate, copies = call(
        aggregate_kernel,
        [((k, v_count), BF), ((n_dp, k, v_count), BF)],
        [arrived, own, slots_row, vectors],
        name="aggregate",
    )
    aggregate_all = swap(copies, "dp").reshape(channels, v_count)

    output, grad_self, spread, payload = call(
        lambda *refs: dense_kernel(scale, cap, *refs),
        [((share, channels), BF), ((share, channels), F32), ((k, v_count), BF), ((n_dom * more, LANES), BF)],
        [
            aggregate_all, self_t, gh_t, w_in, vectors, slots_row, table, aggregate, cotangent, w_out,
            replica,
        ],
        smem=(10,),
        scratch=[
            pltpu.VMEM((channels, v_count), BF),
            pltpu.VMEM((channels, v_count), BF),
            pltpu.VMEM((2, LANES, channels), F32),
        ],
        name="dense",
    )
    arrived = swap(payload, "dom")
    payload, own = edge_pass(arrived, spread, more, True)
    arrived = swap(payload, "dom")
    grad_rows = 2 * 3 * k + k
    (copies,) = call(
        lambda *refs: back_kernel(cap, more, *refs),
        [((n_dp, k + grad_rows, LANES), BF)],
        [arrived, own, slots_row],
        name="back",
    )
    arrived = swap(copies, "dp")
    output, grad_features, grad_w_in, grad_b_in, grad_w_out, grad_b_out = call(
        last_kernel,
        [
            ((share, channels), BF),
            ((share, channels), BF),
            ((2 * channels, channels), F32),
            ((1, channels), F32),
            ((channels, channels), F32),
            ((1, channels), F32),
        ],
        [arrived, grad_self, output, replica],
        smem=(3,),
        scratch=[pltpu.VMEM((LANES, channels), F32)],
        name="last",
    )
    return (output, grad_features, grad_w_in, grad_b_in[0], grad_w_out, grad_b_out[0])


def solution(mesh):
    in_specs = (
        P("dom", None),
        P("dom"),
        P("dom", None, None),
        P("dom", None),
        P("dom", "dp", None, None, None),
        P("dom", "dp", None, None),
        P(),
        P(),
        P(),
        P(),
        P("dom", None),
    )
    out_specs = (P(("dom", "dp"), None), P(("dom", "dp"), None), P(), P(), P(), P())
    return jax.shard_map(
        on_device, mesh=mesh, in_specs=in_specs, out_specs=out_specs, check_vma=False
    )
```

```python
import math

import jax
import jax.numpy as jnp
from jax import lax
from jax.experimental import pallas as pl
from jax.experimental.pallas import tpu as pltpu
from jax.sharding import PartitionSpec as P

BF = jnp.bfloat16
F32 = jnp.float32
LANES = 128
PART = 8
GROUPS = 16
SHIFT = 16


def far(size):
    return size // 2 + size // 8


def turn(rows):
    half = rows.shape[0] // 2
    return jnp.concatenate([rows[half:], rows[:half]], 0)


def matmul(a, b, ca=1, cb=0):
    return lax.dot_general(a, b, (((ca,), (cb,)), ((), ())), preferred_element_type=F32)


def hot(condition):
    return jnp.where(condition, 1.0, 0.0).astype(BF)


def row_choice(slots_row, first, count):
    width = slots_row.shape[1]
    rows = lax.broadcasted_iota(jnp.int32, (count, width), 0)
    return hot(rows == slots_row - first)


def pick(table, slots_row):
    total = None
    for first in range(0, table.shape[1], LANES):
        choice = row_choice(slots_row, first, LANES)
        part = matmul(table[:, first : first + LANES], choice)
        total = part if total is None else total + part
    return total


def scatter(values, slots_row, count):
    parts = []
    for first in range(0, count, LANES):
        choice = row_choice(slots_row, first, LANES)
        parts.append(matmul(values, choice, 1, 1))
    return jnp.concatenate(parts, 1)


def cap_lane(shape, cap):
    return lax.rem(lax.broadcasted_iota(jnp.int32, shape, 1), cap)


def peer_rows(n_rows, per_peer, n_slots, cap):
    rows = lax.broadcasted_iota(jnp.int32, (n_rows, 1), 0)
    part = lax.rem(rows, per_peer)
    used = jnp.where(part < cap // PART, rows // per_peer * (cap // PART) + part, -1)
    slots = lax.broadcasted_iota(jnp.int32, (1, n_slots), 1) // PART
    return hot(slots == used)


def to_peers(columns, per_peer, cap):
    k, n_slots = columns.shape
    n_rows = n_slots // cap * per_peer
    lane = cap_lane(columns.shape, PART)
    spread_out = jnp.concatenate(
        [jnp.where(lane == c, columns, 0.0).astype(BF) for c in range(PART)], 0
    )
    return matmul(peer_rows(n_rows, per_peer, n_slots, cap), spread_out, 1, 1)


def from_peers(arrived, per_peer, cap):
    n_rows, width = arrived.shape
    k = width // PART
    n_slots = n_rows // per_peer * cap
    wide = matmul(arrived, peer_rows(n_rows, per_peer, n_slots, cap), 0, 0)
    lane = cap_lane((k, n_slots), PART)
    total = jnp.zeros((k, n_slots), F32)
    for c in range(PART):
        total = jnp.where(lane == c, wide[c * k : c * k + k], total)
    return total


def to_rows(columns):
    width = columns.shape[1] // PART
    tall = jnp.concatenate([columns[:, c * width : c * width + width] for c in range(PART)], 0)
    return tall.T.astype(BF)


def from_tall(tall):
    k = tall.shape[0] // PART
    return jnp.concatenate([tall[c * k : c * k + k] for c in range(PART)], 1)


def part_rows(n_rows, per_peer, parts):
    n_parts = n_rows // per_peer * parts
    rows = lax.broadcasted_iota(jnp.int32, (n_rows, 1), 0)
    part = lax.rem(rows, per_peer)
    source = jnp.where(part < parts, rows // per_peer * parts + part, -1)
    return hot(lax.broadcasted_iota(jnp.int32, (1, n_parts), 1) == source)


def slots_of(send_rows, send_counts, v_count):
    n_peers, cap = send_rows.shape
    n_slots = n_peers * cap
    parts = cap // PART
    width = n_peers * parts
    slots = lax.broadcasted_iota(jnp.int32, (1, n_slots), 1)
    within = lax.rem(slots, width)
    place = lax.rem(within, parts) * PART + slots // width
    chosen = hot(lax.broadcasted_iota(jnp.int32, (n_peers, 1), 0) == within // parts)
    base = 32
    high = send_rows // base
    low = send_rows - high * base
    both = matmul(high.astype(F32).astype(BF), chosen, 0, 0) * base + matmul(
        low.astype(F32).astype(BF), chosen, 0, 0
    )
    c = lax.broadcasted_iota(jnp.int32, (cap, n_slots), 0)
    rows = jnp.sum(jnp.where(c == place, both, 0.0), 0, keepdims=True)
    counts = jnp.broadcast_to(send_counts.astype(F32), (8, n_peers)).astype(BF)
    counts = matmul(counts, chosen)[:1]
    return jnp.where(place.astype(F32) >= counts, float(v_count), rows).astype(jnp.int32)


def pack_kernel(edges_ref, blocks_ref, copies_ref):
    n_tiles, _, width = edges_ref.shape
    sources, targets = edges_ref[:, 0, :], edges_ref[:, 1, :]
    packed = (targets << SHIFT) + (sources & ((1 << SHIFT) - 1))
    lane = lax.broadcasted_iota(jnp.int32, (n_tiles, width), 1)
    blocks = blocks_ref[...]
    blocks = jnp.where(lane == 0, blocks[:, :1], jnp.where(lane == 1, blocks[:, 1:2], 0))
    for r in range(copies_ref.shape[0]):
        copies_ref[r, :n_tiles, :] = packed
        copies_ref[r, n_tiles:, :] = blocks


def first_kernel(
    features_ref, send_rows_ref, send_counts_ref, replica_ref, table_ref, slots_ref, payload_ref
):
    k, v_count = table_ref.shape
    rows = lax.broadcasted_iota(jnp.int32, (k, features_ref.shape[1]), 0)
    columns = lax.broadcasted_iota(jnp.int32, (k, features_ref.shape[1]), 1)
    mine = hot(columns == rows + replica_ref[0] * k)
    table = matmul(mine, features_ref[...], 1, 1).astype(BF)
    table_ref[...] = table
    slots = slots_of(send_rows_ref[...], send_counts_ref[...], v_count)
    slots_ref[...] = slots
    payload_ref[...] = turn(to_rows(pick(table, slots)))


def inputs_kernel(
    features_ref, cotangent_ref, w_in_ref, b_in_ref, w_out_ref, b_out_ref, degree_ref, self_ref, gh_ref,
    vectors_ref,
):
    w_self = w_in_ref[: features_ref.shape[1], :].astype(F32).T.astype(BF)
    self_ref[...] = matmul(w_self, features_ref[...], 1, 1) + b_in_ref[...].T
    gh_ref[...] = matmul(w_out_ref[...], cotangent_ref[...], 1, 1)
    vectors_ref[...] = jnp.zeros_like(vectors_ref)
    vectors_ref[:1, :] = degree_ref[...].astype(F32)
    vectors_ref[1:2, : b_out_ref.shape[1]] = b_out_ref[...]


def edges_kernel(
    cap, per_peer, transpose, arrived_ref, owned_ref, edges_ref, blocks_ref, ready_ref, payload_ref,
    own_ref, table, total,
):
    del ready_ref
    k, v_count = owned_ref.shape
    own_blocks = v_count // LANES
    all_blocks = table.shape[0]
    arrived = turn(arrived_ref[...])
    mirrors = from_peers(arrived, per_peer, cap)
    owned = owned_ref[...].astype(F32)
    for b in range(own_blocks):
        table[b] = owned[:, b * LANES : b * LANES + LANES]
    for b in range(own_blocks, all_blocks):
        first = (b - own_blocks) * LANES
        table[b] = mirrors[:, first : first + LANES]
    total[...] = jnp.zeros_like(total)
    n_groups, group_rows, width = edges_ref.shape
    per_group = group_rows // 2
    positions = lax.broadcasted_iota(jnp.int32, (LANES, width), 0)
    a, b = (1, 0) if transpose else (0, 1)
    together = math.gcd(n_groups, GROUPS)
    tiles = [(j, t) for j in range(together) for t in range(per_group)]

    def group(i, carry):
        g = i * together

        def slots(tile, side):
            packed = edges_ref[g + tile[0], tile[1] : tile[1] + 1, :]
            return packed >> SHIFT if side else packed & ((1 << SHIFT) - 1)

        def block(tile, side):
            return blocks_ref[g + tile[0], 2 * tile[1] + side]

        gathered = []
        for tile in tiles:
            lanes = jnp.broadcast_to(slots(tile, a) & (LANES - 1), (k, width))
            values = jnp.take_along_axis(table[block(tile, a)], lanes, axis=1, mode="promise_in_bounds")
            gathered.append(values.astype(BF))
        placed = []
        for n in range(0, len(tiles), 2):
            left = jnp.concatenate(gathered[n : n + 2], 0)
            right = jnp.concatenate([hot(positions == slots(tile, b)) for tile in tiles[n : n + 2]], 0)
            product = matmul(left, right, 1, 1)
            placed.extend([product[:k, :LANES], product[k:, LANES:]])
        for tile, values in zip(tiles, placed):
            at = block(tile, b)
            total[at] = total[at] + values
        return carry

    lax.fori_loop(0, n_groups // together, group, 0)
    for b in range(own_blocks):
        own_ref[:, b * LANES : b * LANES + LANES] = total[b]
    back = jnp.concatenate([total[b] for b in range(own_blocks, all_blocks)], 1)
    outgoing = to_peers(back, per_peer, cap)
    if per_peer > cap // PART:
        parts = per_peer - cap // PART
        rows = lax.broadcasted_iota(jnp.int32, (8, arrived.shape[0]), 1)
        part = lax.broadcasted_iota(jnp.int32, (8, arrived.shape[0]), 0)
        chosen = hot(lax.rem(rows, per_peer) == part + cap // PART)
        sums = matmul(chosen, arrived)
        place = lax.rem(lax.broadcasted_iota(jnp.int32, outgoing.shape, 0), per_peer)
        for h in range(parts):
            outgoing = jnp.where(place == cap // PART + h, sums[h : h + 1], outgoing)
    payload_ref[...] = turn(outgoing.astype(BF))


def aggregate_kernel(arrived_ref, own_ref, slots_ref, vectors_ref, aggregate_ref, copies_ref):
    k, v_count = own_ref.shape
    returned = from_tall(turn(arrived_ref[...]).astype(F32).T.astype(BF))
    summed = own_ref[...] + scatter(returned, slots_ref[...], v_count)
    aggregate = (summed / vectors_ref[:1, :]).astype(BF)
    aggregate_ref[...] = aggregate
    for r in range(copies_ref.shape[0]):
        copies_ref[r] = aggregate


def dense_kernel(
    scale, cap, aggregate_ref, self_ref, gh_ref, w_in_ref, vectors_ref, slots_ref, table_ref, mine_ref,
    cotangent_ref, w_out_ref, replica_ref, output_ref, grad_self_ref, spread_ref, payload_ref,
    hidden_ref, grad_pre_ref, rows_ref,
):
    k, v_count = spread_ref.shape
    n_dp = aggregate_ref.shape[0]
    channels = n_dp * k
    aggregate = jnp.concatenate([aggregate_ref[r ^ far(n_dp)] for r in range(n_dp)], 0)
    pre = self_ref[...] + matmul(w_in_ref[channels:, :], aggregate, 0, 0)
    sigmoid = 1.0 / (1.0 + jnp.exp(-pre))
    hidden_ref[...] = (pre * sigmoid).astype(BF)
    grad_pre = (gh_ref[...] * (sigmoid * (1.0 + pre * (1.0 - sigmoid)))).astype(BF)
    grad_pre_ref[...] = grad_pre
    share = output_ref.shape[0]
    per_block = LANES // share
    block = pl.multiple_of((replica_ref[0] // per_block) * LANES, LANES)
    half = pl.multiple_of(lax.rem(replica_ref[0], per_block) * share, share)
    rows_ref[0] = matmul(hidden_ref[:, pl.ds(block, LANES)], w_out_ref[...], 0, 0)
    output_ref[...] = (rows_ref[0, pl.ds(half, share), :] + vectors_ref[1:2, :channels]).astype(BF)
    rows_ref[1] = matmul(w_in_ref[:channels, :], grad_pre_ref[:, pl.ds(block, LANES)]).T
    grad_self_ref[...] = rows_ref[1, pl.ds(half, share), :]
    first = pl.multiple_of(replica_ref[0] * k, k)
    spread = matmul(w_in_ref[pl.ds(pl.multiple_of(channels + first, k), k), :], grad_pre)
    spread = (spread / vectors_ref[:1, :]).astype(BF)
    spread_ref[...] = spread

    ones = jnp.ones((k, v_count), BF)
    left = jnp.concatenate([table_ref[...], mine_ref[...], ones], 0)
    grads_in = (matmul(left, grad_pre, 1, 1) * scale).astype(BF)
    left = jnp.concatenate([hidden_ref[pl.ds(first, k), :], ones], 0)
    grads_out = (matmul(left, cotangent_ref[...]) * scale).astype(BF)
    grads = jnp.concatenate([grads_in[: 2 * k], grads_out[:k], grads_in[2 * k :], grads_out[k:]], 0)

    parts = cap // PART
    halves = channels // LANES
    per_peer = parts + halves
    picked = to_rows(pick(spread, slots_ref[...]))
    n_rows = picked.shape[0] // parts * per_peer
    payload = matmul(part_rows(n_rows, per_peer, parts), picked)
    rows = lax.broadcasted_iota(jnp.int32, (n_rows, grads.shape[0]), 0)
    source = lax.broadcasted_iota(jnp.int32, (n_rows, grads.shape[0]), 1)
    peer = jnp.where(source == 4 * k, 3 * k + 1, jnp.where(source > 3 * k, -1, source))
    for h in range(halves):
        chosen = hot((rows // per_peer == peer) & (lax.rem(rows, per_peer) == parts + h))
        payload = payload + matmul(chosen, grads[:, h * LANES : h * LANES + LANES])
    payload_ref[...] = turn(payload.astype(BF))


def back_kernel(cap, per_peer, arrived_ref, own_ref, slots_ref, copies_ref):
    k, v_count = own_ref.shape
    n_dp = copies_ref.shape[0]
    share = v_count // n_dp
    arrived = turn(arrived_ref[...])
    tall = matmul(arrived, part_rows(arrived.shape[0], per_peer, cap // PART), 0, 0)
    returned = from_tall(tall.astype(BF))
    summed = (own_ref[...] + scatter(returned, slots_ref[...], v_count)).astype(BF)
    n_rows = copies_ref.shape[1] - k
    parts = cap // PART
    halves = per_peer - parts
    to = lax.broadcasted_iota(jnp.int32, (n_rows, arrived.shape[0]), 0)
    source = lax.broadcasted_iota(jnp.int32, (n_rows, arrived.shape[0]), 1)
    peer, half = source // per_peer, lax.rem(source, per_peer) - parts
    place = jnp.where(peer < 3 * k, half * (3 * k) + peer, halves * 3 * k + (peer - 3 * k) * halves + half)
    chosen = hot((place == to) & (half >= 0))
    grads = matmul(chosen, arrived).astype(BF)
    for r in range(n_dp):
        first = r * share // LANES * LANES
        copies_ref[r ^ far(n_dp), :k] = summed[:, first : first + LANES]
        copies_ref[r ^ far(n_dp), k:] = grads


def last_kernel(
    arrived_ref, grad_self_ref, rows_out_ref, replica_ref, output_ref, grad_features_ref, grad_w_in_ref,
    grad_b_in_ref, grad_w_out_ref, grad_b_out_ref, rows_ref,
):
    output_ref[...] = rows_out_ref[...]
    share, channels = grad_features_ref.shape
    n_dp = arrived_ref.shape[0]
    k = channels // n_dp
    half = pl.multiple_of(lax.rem(replica_ref[0], LANES // share) * share, share)
    columns = jnp.concatenate([arrived_ref[r ^ far(n_dp), :k] for r in range(n_dp)], 0)
    rows_ref[...] = columns.astype(F32).T
    grad_features_ref[...] = (rows_ref[pl.ds(half, share), :] + grad_self_ref[...]).astype(BF)
    halves = channels // LANES
    for h in range(halves):
        lanes = slice(h * LANES, h * LANES + LANES)
        first = k + h * 3 * k
        for r in range(n_dp):
            rows = slice(r * k, r * k + k)
            grad_w_in_ref[rows, lanes] = arrived_ref[r ^ far(n_dp), first : first + k].astype(F32)
            second = slice(channels + r * k, channels + r * k + k)
            grad_w_in_ref[second, lanes] = arrived_ref[r ^ far(n_dp), first + k : first + 2 * k].astype(F32)
            grad_w_out_ref[rows, lanes] = arrived_ref[r ^ far(n_dp), first + 2 * k : first + 3 * k].astype(F32)
        biases = arrived_ref[0, k + halves * 3 * k :].astype(F32)
        grad_b_in_ref[:, lanes] = biases[h : h + 1]
        grad_b_out_ref[:, lanes] = biases[halves + h : halves + h + 1]


def call(kernel, outs, args, smem=(), scratch=(), flops=0, name=None):
    in_specs = [
        pl.BlockSpec(memory_space=pltpu.SMEM if i in smem else pltpu.VMEM) for i in range(len(args))
    ]
    shapes = [jax.ShapeDtypeStruct(s, d) for s, d in outs]
    size = sum(math.prod(s) * jnp.dtype(d).itemsize for s, d in outs)
    size += sum(x.size * x.dtype.itemsize for x in args)
    return pl.pallas_call(
        kernel,
        out_shape=shapes,
        in_specs=in_specs,
        out_specs=[pl.BlockSpec(memory_space=pltpu.VMEM) for _ in outs],
        scratch_shapes=list(scratch),
        compiler_params=pltpu.CompilerParams(vmem_limit_bytes=8 * 1024 * 1024),
        cost_estimate=pl.CostEstimate(flops=flops, bytes_accessed=size, transcendentals=0),
        name=name,
    )(*args)


def swap(values, axis):
    size = lax.axis_size(axis)
    if axis == "dom":
        group = [(i + size // 2) % size for i in range(size)]
    else:
        group = [i ^ far(size) for i in range(size)]
    return lax.all_to_all(values, axis, split_axis=0, concat_axis=0, axis_index_groups=[group], tiled=True)


def on_device(
    features,
    degree,
    send_rows,
    send_counts,
    edge_slots,
    tile_blocks,
    w_in,
    b_in,
    w_out,
    b_out,
    cotangent,
):
    n_dp = lax.axis_size("dp")
    n_dom = lax.axis_size("dom")
    replica = lax.axis_index("dp").astype(jnp.int32).reshape(1)
    v_count, channels = features.shape
    cap = send_rows.shape[2]
    k = channels // n_dp
    share = v_count // n_dp
    n_slots = n_dom * cap
    n_tiles, _, tile_rows = edge_slots.shape[2:]
    blocks_count = (v_count + n_slots) // LANES
    scale = 1.0 / math.sqrt(v_count * n_dom)

    parts = cap // PART
    more = parts + channels // LANES

    (edges,) = call(
        pack_kernel,
        [((n_dp, 2 * n_tiles, tile_rows), jnp.int32)],
        [edge_slots[0, 0], tile_blocks[0, 0]],
        name="pack",
    )
    edges = swap(edges, "dp")
    blocks = edges[:, n_tiles:, :2].reshape(n_dp, 2 * n_tiles)

    table, slots_row, payload = call(
        first_kernel,
        [((k, v_count), BF), ((1, n_slots), jnp.int32), ((n_dom * parts, LANES), BF)],
        [features, send_rows[0], send_counts, replica],
        smem=(3,),
        name="first",
    )
    arrived = swap(payload, "dom")
    self_t, gh_t, vectors = call(
        inputs_kernel,
        [((channels, v_count), F32), ((channels, v_count), F32), ((8, v_count), F32)],
        [
            features, cotangent, w_in, b_in.reshape(1, -1), w_out, b_out.reshape(1, -1),
            degree.reshape(1, v_count),
        ],
        name="inputs",
    )

    def edge_pass(arrived, owned, per_peer, transpose):
        return call(
            lambda *refs: edges_kernel(cap, per_peer, transpose, *refs),
            [((n_dom * per_peer, LANES), BF), ((k, v_count), F32)],
            [arrived, owned, edges, blocks, vectors],
            smem=(3,),
            scratch=[
                pltpu.VMEM((blocks_count, k, LANES), F32),
                pltpu.VMEM((blocks_count, k, LANES), F32),
            ],
            name="edges_back" if transpose else "edges",
        )

    payload, own = edge_pass(arrived, table, parts, False)
    arrived = swap(payload, "dom")
    aggregate, copies = call(
        aggregate_kernel,
        [((k, v_count), BF), ((n_dp, k, v_count), BF)],
        [arrived, own, slots_row, vectors],
        name="aggregate",
    )
    aggregate_all = swap(copies, "dp")

    output, grad_self, spread, payload = call(
        lambda *refs: dense_kernel(scale, cap, *refs),
        [((share, channels), BF), ((share, channels), F32), ((k, v_count), BF), ((n_dom * more, LANES), BF)],
        [
            aggregate_all, self_t, gh_t, w_in, vectors, slots_row, table, aggregate, cotangent, w_out,
            replica,
        ],
        smem=(10,),
        scratch=[
            pltpu.VMEM((channels, v_count), BF),
            pltpu.VMEM((channels, v_count), BF),
            pltpu.VMEM((2, LANES, channels), F32),
        ],
        name="dense",
    )
    arrived = swap(payload, "dom")
    payload, own = edge_pass(arrived, spread, more, True)
    arrived = swap(payload, "dom")
    grad_rows = 2 * 3 * k + k
    (copies,) = call(
        lambda *refs: back_kernel(cap, more, *refs),
        [((n_dp, k + grad_rows, LANES), BF)],
        [arrived, own, slots_row],
        name="back",
    )
    arrived = swap(copies, "dp")
    output, grad_features, grad_w_in, grad_b_in, grad_w_out, grad_b_out = call(
        last_kernel,
        [
            ((share, channels), BF),
            ((share, channels), BF),
            ((2 * channels, channels), F32),
            ((1, channels), F32),
            ((channels, channels), F32),
            ((1, channels), F32),
        ],
        [arrived, grad_self, output, replica],
        smem=(3,),
        scratch=[pltpu.VMEM((LANES, channels), F32)],
        name="last",
    )
    return (output, grad_features, grad_w_in, grad_b_in[0], grad_w_out, grad_b_out[0])


def solution(mesh):
    in_specs = (
        P("dom", None),
        P("dom"),
        P("dom", None, None),
        P("dom", None),
        P("dom", "dp", None, None, None),
        P("dom", "dp", None, None),
        P(),
        P(),
        P(),
        P(),
        P("dom", None),
    )
    out_specs = (P(("dom", "dp"), None), P(("dom", "dp"), None), P(), P(), P(), P())
    return jax.shard_map(
        on_device, mesh=mesh, in_specs=in_specs, out_specs=out_specs, check_vma=False
    )
```

```python
import math

import jax
import jax.numpy as jnp
from jax import lax
from jax.experimental import pallas as pl
from jax.experimental.pallas import tpu as pltpu
from jax.sharding import PartitionSpec as P

BF = jnp.bfloat16
F32 = jnp.float32
LANES = 128
PART = 8
GROUPS = 16
SHIFT = 16
STRIDE = 33


def far(size):
    return size // 2 + size // 8


def peer_at(position, size):
    return (size // 2 + STRIDE * position) % size


def matmul(a, b, ca=1, cb=0):
    return lax.dot_general(a, b, (((ca,), (cb,)), ((), ())), preferred_element_type=F32)


def hot(condition):
    return jnp.where(condition, 1.0, 0.0).astype(BF)


def row_choice(slots_row, first, count):
    width = slots_row.shape[1]
    rows = lax.broadcasted_iota(jnp.int32, (count, width), 0)
    return hot(rows == slots_row - first)


def pick(table, slots_row):
    total = None
    for first in range(0, table.shape[1], LANES):
        choice = row_choice(slots_row, first, LANES)
        part = matmul(table[:, first : first + LANES], choice)
        total = part if total is None else total + part
    return total


def scatter(values, slots_row, count):
    parts = []
    for first in range(0, count, LANES):
        choice = row_choice(slots_row, first, LANES)
        parts.append(matmul(values, choice, 1, 1))
    return jnp.concatenate(parts, 1)


def cap_lane(shape, cap):
    return lax.rem(lax.broadcasted_iota(jnp.int32, shape, 1), cap)


def peer_rows(n_rows, per_peer, n_slots, cap):
    rows = lax.broadcasted_iota(jnp.int32, (n_rows, 1), 0)
    part = lax.rem(rows, per_peer)
    peer = peer_at(rows // per_peer, n_rows // per_peer)
    used = jnp.where(part < cap // PART, peer * (cap // PART) + part, -1)
    slots = lax.broadcasted_iota(jnp.int32, (1, n_slots), 1) // PART
    return hot(slots == used)


def to_peers(columns, per_peer, cap):
    k, n_slots = columns.shape
    n_rows = n_slots // cap * per_peer
    lane = cap_lane(columns.shape, PART)
    spread_out = jnp.concatenate(
        [jnp.where(lane == c, columns, 0.0).astype(BF) for c in range(PART)], 0
    )
    return matmul(peer_rows(n_rows, per_peer, n_slots, cap), spread_out, 1, 1)


def from_peers(arrived, per_peer, cap):
    n_rows, width = arrived.shape
    k = width // PART
    n_slots = n_rows // per_peer * cap
    wide = matmul(arrived, peer_rows(n_rows, per_peer, n_slots, cap), 0, 0)
    lane = cap_lane((k, n_slots), PART)
    total = jnp.zeros((k, n_slots), F32)
    for c in range(PART):
        total = jnp.where(lane == c, wide[c * k : c * k + k], total)
    return total


def to_rows(columns):
    width = columns.shape[1] // PART
    tall = jnp.concatenate([columns[:, c * width : c * width + width] for c in range(PART)], 0)
    return tall.T.astype(BF)


def from_tall(tall):
    k = tall.shape[0] // PART
    return jnp.concatenate([tall[c * k : c * k + k] for c in range(PART)], 1)


def part_rows(n_rows, per_peer, parts):
    n_parts = n_rows // per_peer * parts
    rows = lax.broadcasted_iota(jnp.int32, (n_rows, 1), 0)
    part = lax.rem(rows, per_peer)
    source = jnp.where(part < parts, rows // per_peer * parts + part, -1)
    return hot(lax.broadcasted_iota(jnp.int32, (1, n_parts), 1) == source)


def slots_of(send_rows, send_counts, v_count):
    n_peers, cap = send_rows.shape
    n_slots = n_peers * cap
    parts = cap // PART
    width = n_peers * parts
    slots = lax.broadcasted_iota(jnp.int32, (1, n_slots), 1)
    within = lax.rem(slots, width)
    place = lax.rem(within, parts) * PART + slots // width
    chosen = hot(lax.broadcasted_iota(jnp.int32, (n_peers, 1), 0) == peer_at(within // parts, n_peers))
    base = 32
    high = send_rows // base
    low = send_rows - high * base
    both = matmul(high.astype(F32).astype(BF), chosen, 0, 0) * base + matmul(
        low.astype(F32).astype(BF), chosen, 0, 0
    )
    c = lax.broadcasted_iota(jnp.int32, (cap, n_slots), 0)
    rows = jnp.sum(jnp.where(c == place, both, 0.0), 0, keepdims=True)
    counts = jnp.broadcast_to(send_counts.astype(F32), (8, n_peers)).astype(BF)
    counts = matmul(counts, chosen)[:1]
    return jnp.where(place.astype(F32) >= counts, float(v_count), rows).astype(jnp.int32)


def pack_kernel(edges_ref, blocks_ref, copies_ref):
    n_tiles, _, width = edges_ref.shape
    sources, targets = edges_ref[:, 0, :], edges_ref[:, 1, :]
    packed = (targets << SHIFT) + (sources & ((1 << SHIFT) - 1))
    lane = lax.broadcasted_iota(jnp.int32, (n_tiles, width), 1)
    blocks = blocks_ref[...]
    blocks = jnp.where(lane == 0, blocks[:, :1], jnp.where(lane == 1, blocks[:, 1:2], 0))
    for r in range(copies_ref.shape[0]):
        copies_ref[r, :n_tiles, :] = packed
        copies_ref[r, n_tiles:, :] = blocks


def first_kernel(
    features_ref, send_rows_ref, send_counts_ref, replica_ref, table_ref, slots_ref, payload_ref
):
    k, v_count = table_ref.shape
    rows = lax.broadcasted_iota(jnp.int32, (k, features_ref.shape[1]), 0)
    columns = lax.broadcasted_iota(jnp.int32, (k, features_ref.shape[1]), 1)
    mine = hot(columns == rows + replica_ref[0] * k)
    table = matmul(mine, features_ref[...], 1, 1).astype(BF)
    table_ref[...] = table
    slots = slots_of(send_rows_ref[...], send_counts_ref[...], v_count)
    slots_ref[...] = slots
    payload_ref[...] = to_rows(pick(table, slots))


def inputs_kernel(
    features_ref, cotangent_ref, w_in_ref, b_in_ref, w_out_ref, b_out_ref, degree_ref, self_ref, gh_ref,
    vectors_ref,
):
    w_self = w_in_ref[: features_ref.shape[1], :].astype(F32).T.astype(BF)
    self_ref[...] = matmul(w_self, features_ref[...], 1, 1) + b_in_ref[...].T
    gh_ref[...] = matmul(w_out_ref[...], cotangent_ref[...], 1, 1)
    vectors_ref[...] = jnp.zeros_like(vectors_ref)
    vectors_ref[:1, :] = degree_ref[...].astype(F32)
    vectors_ref[1:2, : b_out_ref.shape[1]] = b_out_ref[...]


def edges_kernel(
    cap, per_peer, transpose, arrived_ref, owned_ref, edges_ref, blocks_ref, ready_ref, payload_ref,
    own_ref, table, total,
):
    del ready_ref
    k, v_count = owned_ref.shape
    own_blocks = v_count // LANES
    all_blocks = table.shape[0]
    arrived = arrived_ref[...]
    mirrors = from_peers(arrived, per_peer, cap)
    owned = owned_ref[...].astype(F32)
    for b in range(own_blocks):
        table[b] = owned[:, b * LANES : b * LANES + LANES]
    for b in range(own_blocks, all_blocks):
        first = (b - own_blocks) * LANES
        table[b] = mirrors[:, first : first + LANES]
    total[...] = jnp.zeros_like(total)
    n_groups, group_rows, width = edges_ref.shape
    per_group = group_rows // 2
    positions = lax.broadcasted_iota(jnp.int32, (LANES, width), 0)
    a, b = (1, 0) if transpose else (0, 1)
    together = math.gcd(n_groups, GROUPS)
    tiles = [(j, t) for j in range(together) for t in range(per_group)]

    def group(i, carry):
        g = i * together

        def slots(tile, side):
            packed = edges_ref[g + tile[0], tile[1] : tile[1] + 1, :]
            return packed >> SHIFT if side else packed & ((1 << SHIFT) - 1)

        def block(tile, side):
            return blocks_ref[g + tile[0], 2 * tile[1] + side]

        gathered = []
        for tile in tiles:
            lanes = jnp.broadcast_to(slots(tile, a) & (LANES - 1), (k, width))
            values = jnp.take_along_axis(table[block(tile, a)], lanes, axis=1, mode="promise_in_bounds")
            gathered.append(values.astype(BF))
        placed = []
        for n in range(0, len(tiles), 2):
            left = jnp.concatenate(gathered[n : n + 2], 0)
            right = jnp.concatenate([hot(positions == slots(tile, b)) for tile in tiles[n : n + 2]], 0)
            product = matmul(left, right, 1, 1)
            placed.extend([product[:k, :LANES], product[k:, LANES:]])
        for tile, values in zip(tiles, placed):
            at = block(tile, b)
            total[at] = total[at] + values
        return carry

    lax.fori_loop(0, n_groups // together, group, 0)
    for b in range(own_blocks):
        own_ref[:, b * LANES : b * LANES + LANES] = total[b]
    back = jnp.concatenate([total[b] for b in range(own_blocks, all_blocks)], 1)
    outgoing = to_peers(back, per_peer, cap)
    if per_peer > cap // PART:
        parts = per_peer - cap // PART
        rows = lax.broadcasted_iota(jnp.int32, (8, arrived.shape[0]), 1)
        part = lax.broadcasted_iota(jnp.int32, (8, arrived.shape[0]), 0)
        chosen = hot(lax.rem(rows, per_peer) == part + cap // PART)
        sums = matmul(chosen, arrived)
        place = lax.rem(lax.broadcasted_iota(jnp.int32, outgoing.shape, 0), per_peer)
        for h in range(parts):
            outgoing = jnp.where(place == cap // PART + h, sums[h : h + 1], outgoing)
    payload_ref[...] = outgoing.astype(BF)


def aggregate_kernel(arrived_ref, own_ref, slots_ref, vectors_ref, aggregate_ref, copies_ref):
    k, v_count = own_ref.shape
    returned = from_tall(arrived_ref[...].astype(F32).T.astype(BF))
    summed = own_ref[...] + scatter(returned, slots_ref[...], v_count)
    aggregate = (summed / vectors_ref[:1, :]).astype(BF)
    aggregate_ref[...] = aggregate
    for r in range(copies_ref.shape[0]):
        copies_ref[r] = aggregate


def dense_kernel(
    scale, cap, aggregate_ref, self_ref, gh_ref, w_in_ref, vectors_ref, slots_ref, table_ref, mine_ref,
    cotangent_ref, w_out_ref, replica_ref, output_ref, grad_self_ref, spread_ref, payload_ref,
    hidden_ref, grad_pre_ref, rows_ref,
):
    k, v_count = spread_ref.shape
    n_dp = aggregate_ref.shape[0]
    channels = n_dp * k
    aggregate = jnp.concatenate([aggregate_ref[r ^ far(n_dp)] for r in range(n_dp)], 0)
    pre = self_ref[...] + matmul(w_in_ref[channels:, :], aggregate, 0, 0)
    sigmoid = 1.0 / (1.0 + jnp.exp(-pre))
    hidden_ref[...] = (pre * sigmoid).astype(BF)
    grad_pre = (gh_ref[...] * (sigmoid * (1.0 + pre * (1.0 - sigmoid)))).astype(BF)
    grad_pre_ref[...] = grad_pre
    share = output_ref.shape[0]
    per_block = LANES // share
    block = pl.multiple_of((replica_ref[0] // per_block) * LANES, LANES)
    half = pl.multiple_of(lax.rem(replica_ref[0], per_block) * share, share)
    rows_ref[0] = matmul(hidden_ref[:, pl.ds(block, LANES)], w_out_ref[...], 0, 0)
    output_ref[...] = (rows_ref[0, pl.ds(half, share), :] + vectors_ref[1:2, :channels]).astype(BF)
    rows_ref[1] = matmul(w_in_ref[:channels, :], grad_pre_ref[:, pl.ds(block, LANES)]).T
    grad_self_ref[...] = rows_ref[1, pl.ds(half, share), :]
    first = pl.multiple_of(replica_ref[0] * k, k)
    spread = matmul(w_in_ref[pl.ds(pl.multiple_of(channels + first, k), k), :], grad_pre)
    spread = (spread / vectors_ref[:1, :]).astype(BF)
    spread_ref[...] = spread

    ones = jnp.ones((k, v_count), BF)
    left = jnp.concatenate([table_ref[...], mine_ref[...], ones], 0)
    grads_in = (matmul(left, grad_pre, 1, 1) * scale).astype(BF)
    left = jnp.concatenate([hidden_ref[pl.ds(first, k), :], ones], 0)
    grads_out = (matmul(left, cotangent_ref[...]) * scale).astype(BF)
    grads = jnp.concatenate([grads_in[: 2 * k], grads_out[:k], grads_in[2 * k :], grads_out[k:]], 0)

    parts = cap // PART
    halves = channels // LANES
    per_peer = parts + halves
    picked = to_rows(pick(spread, slots_ref[...]))
    n_rows = picked.shape[0] // parts * per_peer
    payload = matmul(part_rows(n_rows, per_peer, parts), picked)
    rows = lax.broadcasted_iota(jnp.int32, (n_rows, grads.shape[0]), 0)
    source = lax.broadcasted_iota(jnp.int32, (n_rows, grads.shape[0]), 1)
    peer = jnp.where(source == 4 * k, 3 * k + 1, jnp.where(source > 3 * k, -1, source))
    for h in range(halves):
        chosen = hot((peer_at(rows // per_peer, n_rows // per_peer) == peer) & (lax.rem(rows, per_peer) == parts + h))
        payload = payload + matmul(chosen, grads[:, h * LANES : h * LANES + LANES])
    payload_ref[...] = payload.astype(BF)


def back_kernel(cap, per_peer, arrived_ref, own_ref, slots_ref, copies_ref):
    k, v_count = own_ref.shape
    n_dp = copies_ref.shape[0]
    share = v_count // n_dp
    arrived = arrived_ref[...]
    tall = matmul(arrived, part_rows(arrived.shape[0], per_peer, cap // PART), 0, 0)
    returned = from_tall(tall.astype(BF))
    summed = (own_ref[...] + scatter(returned, slots_ref[...], v_count)).astype(BF)
    n_rows = copies_ref.shape[1] - k
    parts = cap // PART
    halves = per_peer - parts
    to = lax.broadcasted_iota(jnp.int32, (n_rows, arrived.shape[0]), 0)
    source = lax.broadcasted_iota(jnp.int32, (n_rows, arrived.shape[0]), 1)
    peer = peer_at(source // per_peer, arrived.shape[0] // per_peer)
    half = lax.rem(source, per_peer) - parts
    place = jnp.where(peer < 3 * k, half * (3 * k) + peer, halves * 3 * k + (peer - 3 * k) * halves + half)
    chosen = hot((place == to) & (half >= 0))
    grads = matmul(chosen, arrived).astype(BF)
    for r in range(n_dp):
        first = r * share // LANES * LANES
        copies_ref[r ^ far(n_dp), :k] = summed[:, first : first + LANES]
        copies_ref[r ^ far(n_dp), k:] = grads


def last_kernel(
    arrived_ref, grad_self_ref, rows_out_ref, replica_ref, output_ref, grad_features_ref, grad_w_in_ref,
    grad_b_in_ref, grad_w_out_ref, grad_b_out_ref, rows_ref,
):
    output_ref[...] = rows_out_ref[...]
    share, channels = grad_features_ref.shape
    n_dp = arrived_ref.shape[0]
    k = channels // n_dp
    half = pl.multiple_of(lax.rem(replica_ref[0], LANES // share) * share, share)
    columns = jnp.concatenate([arrived_ref[r ^ far(n_dp), :k] for r in range(n_dp)], 0)
    rows_ref[...] = columns.astype(F32).T
    grad_features_ref[...] = (rows_ref[pl.ds(half, share), :] + grad_self_ref[...]).astype(BF)
    halves = channels // LANES
    for h in range(halves):
        lanes = slice(h * LANES, h * LANES + LANES)
        first = k + h * 3 * k
        for r in range(n_dp):
            rows = slice(r * k, r * k + k)
            grad_w_in_ref[rows, lanes] = arrived_ref[r ^ far(n_dp), first : first + k].astype(F32)
            second = slice(channels + r * k, channels + r * k + k)
            grad_w_in_ref[second, lanes] = arrived_ref[r ^ far(n_dp), first + k : first + 2 * k].astype(F32)
            grad_w_out_ref[rows, lanes] = arrived_ref[r ^ far(n_dp), first + 2 * k : first + 3 * k].astype(F32)
        biases = arrived_ref[0, k + halves * 3 * k :].astype(F32)
        grad_b_in_ref[:, lanes] = biases[h : h + 1]
        grad_b_out_ref[:, lanes] = biases[halves + h : halves + h + 1]


def call(kernel, outs, args, smem=(), scratch=(), flops=0, name=None):
    in_specs = [
        pl.BlockSpec(memory_space=pltpu.SMEM if i in smem else pltpu.VMEM) for i in range(len(args))
    ]
    shapes = [jax.ShapeDtypeStruct(s, d) for s, d in outs]
    size = sum(math.prod(s) * jnp.dtype(d).itemsize for s, d in outs)
    size += sum(x.size * x.dtype.itemsize for x in args)
    return pl.pallas_call(
        kernel,
        out_shape=shapes,
        in_specs=in_specs,
        out_specs=[pl.BlockSpec(memory_space=pltpu.VMEM) for _ in outs],
        scratch_shapes=list(scratch),
        compiler_params=pltpu.CompilerParams(vmem_limit_bytes=8 * 1024 * 1024),
        cost_estimate=pl.CostEstimate(flops=flops, bytes_accessed=size, transcendentals=0),
        name=name,
    )(*args)


def swap(values, axis):
    size = lax.axis_size(axis)
    if axis == "dom":
        group = [peer_at(i, size) for i in range(size)]
    else:
        group = [i ^ far(size) for i in range(size)]
    return lax.all_to_all(values, axis, split_axis=0, concat_axis=0, axis_index_groups=[group], tiled=True)


def on_device(
    features,
    degree,
    send_rows,
    send_counts,
    edge_slots,
    tile_blocks,
    w_in,
    b_in,
    w_out,
    b_out,
    cotangent,
):
    n_dp = lax.axis_size("dp")
    n_dom = lax.axis_size("dom")
    replica = lax.axis_index("dp").astype(jnp.int32).reshape(1)
    v_count, channels = features.shape
    cap = send_rows.shape[2]
    k = channels // n_dp
    share = v_count // n_dp
    n_slots = n_dom * cap
    n_tiles, _, tile_rows = edge_slots.shape[2:]
    blocks_count = (v_count + n_slots) // LANES
    scale = 1.0 / math.sqrt(v_count * n_dom)

    parts = cap // PART
    more = parts + channels // LANES

    (edges,) = call(
        pack_kernel,
        [((n_dp, 2 * n_tiles, tile_rows), jnp.int32)],
        [edge_slots[0, 0], tile_blocks[0, 0]],
        name="pack",
    )
    edges = swap(edges, "dp")
    blocks = edges[:, n_tiles:, :2].reshape(n_dp, 2 * n_tiles)

    table, slots_row, payload = call(
        first_kernel,
        [((k, v_count), BF), ((1, n_slots), jnp.int32), ((n_dom * parts, LANES), BF)],
        [features, send_rows[0], send_counts, replica],
        smem=(3,),
        name="first",
    )
    arrived = swap(payload, "dom")
    self_t, gh_t, vectors = call(
        inputs_kernel,
        [((channels, v_count), F32), ((channels, v_count), F32), ((8, v_count), F32)],
        [
            features, cotangent, w_in, b_in.reshape(1, -1), w_out, b_out.reshape(1, -1),
            degree.reshape(1, v_count),
        ],
        name="inputs",
    )

    def edge_pass(arrived, owned, per_peer, transpose):
        return call(
            lambda *refs: edges_kernel(cap, per_peer, transpose, *refs),
            [((n_dom * per_peer, LANES), BF), ((k, v_count), F32)],
            [arrived, owned, edges, blocks, vectors],
            smem=(3,),
            scratch=[
                pltpu.VMEM((blocks_count, k, LANES), F32),
                pltpu.VMEM((blocks_count, k, LANES), F32),
            ],
            name="edges_back" if transpose else "edges",
        )

    payload, own = edge_pass(arrived, table, parts, False)
    arrived = swap(payload, "dom")
    aggregate, copies = call(
        aggregate_kernel,
        [((k, v_count), BF), ((n_dp, k, v_count), BF)],
        [arrived, own, slots_row, vectors],
        name="aggregate",
    )
    aggregate_all = swap(copies, "dp")

    output, grad_self, spread, payload = call(
        lambda *refs: dense_kernel(scale, cap, *refs),
        [((share, channels), BF), ((share, channels), F32), ((k, v_count), BF), ((n_dom * more, LANES), BF)],
        [
            aggregate_all, self_t, gh_t, w_in, vectors, slots_row, table, aggregate, cotangent, w_out,
            replica,
        ],
        smem=(10,),
        scratch=[
            pltpu.VMEM((channels, v_count), BF),
            pltpu.VMEM((channels, v_count), BF),
            pltpu.VMEM((2, LANES, channels), F32),
        ],
        name="dense",
    )
    arrived = swap(payload, "dom")
    payload, own = edge_pass(arrived, spread, more, True)
    arrived = swap(payload, "dom")
    grad_rows = 2 * 3 * k + k
    (copies,) = call(
        lambda *refs: back_kernel(cap, more, *refs),
        [((n_dp, k + grad_rows, LANES), BF)],
        [arrived, own, slots_row],
        name="back",
    )
    arrived = swap(copies, "dp")
    output, grad_features, grad_w_in, grad_b_in, grad_w_out, grad_b_out = call(
        last_kernel,
        [
            ((share, channels), BF),
            ((share, channels), BF),
            ((2 * channels, channels), F32),
            ((1, channels), F32),
            ((channels, channels), F32),
            ((1, channels), F32),
        ],
        [arrived, grad_self, output, replica],
        smem=(3,),
        scratch=[pltpu.VMEM((LANES, channels), F32)],
        name="last",
    )
    return (output, grad_features, grad_w_in, grad_b_in[0], grad_w_out, grad_b_out[0])


def solution(mesh):
    in_specs = (
        P("dom", None),
        P("dom"),
        P("dom", None, None),
        P("dom", None),
        P("dom", "dp", None, None, None),
        P("dom", "dp", None, None),
        P(),
        P(),
        P(),
        P(),
        P("dom", None),
    )
    out_specs = (P(("dom", "dp"), None), P(("dom", "dp"), None), P(), P(), P(), P())
    return jax.shard_map(
        on_device, mesh=mesh, in_specs=in_specs, out_specs=out_specs, check_vma=False
    )
```

```python
import math

import jax
import jax.numpy as jnp
from jax import lax
from jax.experimental import pallas as pl
from jax.experimental.pallas import tpu as pltpu
from jax.sharding import PartitionSpec as P

BF = jnp.bfloat16
F32 = jnp.float32
LANES = 128
PART = 8
GROUPS = 16
SHIFT = 16
STRIDE = 33


def far(size):
    return size // 2 + size // 8


def replica_at(position, size):
    return (far(size) + (size // 2 + 1) * position) % size


def place_of(replica, size):
    return ((size // 2 + 1) * (replica - far(size))) % size


def peer_at(position, size):
    return (size // 2 + STRIDE * position) % size


def matmul(a, b, ca=1, cb=0):
    return lax.dot_general(a, b, (((ca,), (cb,)), ((), ())), preferred_element_type=F32)


def hot(condition):
    return jnp.where(condition, 1.0, 0.0).astype(BF)


def row_choice(slots_row, first, count):
    width = slots_row.shape[1]
    rows = lax.broadcasted_iota(jnp.int32, (count, width), 0)
    return hot(rows == slots_row - first)


def pick(table, slots_row):
    total = None
    for first in range(0, table.shape[1], LANES):
        choice = row_choice(slots_row, first, LANES)
        part = matmul(table[:, first : first + LANES], choice)
        total = part if total is None else total + part
    return total


def scatter(values, slots_row, count):
    parts = []
    for first in range(0, count, LANES):
        choice = row_choice(slots_row, first, LANES)
        parts.append(matmul(values, choice, 1, 1))
    return jnp.concatenate(parts, 1)


def cap_lane(shape, cap):
    return lax.rem(lax.broadcasted_iota(jnp.int32, shape, 1), cap)


def peer_rows(n_rows, per_peer, n_slots, cap):
    rows = lax.broadcasted_iota(jnp.int32, (n_rows, 1), 0)
    part = lax.rem(rows, per_peer)
    peer = peer_at(rows // per_peer, n_rows // per_peer)
    used = jnp.where(part < cap // PART, peer * (cap // PART) + part, -1)
    slots = lax.broadcasted_iota(jnp.int32, (1, n_slots), 1) // PART
    return hot(slots == used)


def to_peers(columns, per_peer, cap):
    k, n_slots = columns.shape
    n_rows = n_slots // cap * per_peer
    lane = cap_lane(columns.shape, PART)
    spread_out = jnp.concatenate(
        [jnp.where(lane == c, columns, 0.0).astype(BF) for c in range(PART)], 0
    )
    return matmul(peer_rows(n_rows, per_peer, n_slots, cap), spread_out, 1, 1)


def from_peers(arrived, per_peer, cap):
    n_rows, width = arrived.shape
    k = width // PART
    n_slots = n_rows // per_peer * cap
    wide = matmul(arrived, peer_rows(n_rows, per_peer, n_slots, cap), 0, 0)
    lane = cap_lane((k, n_slots), PART)
    total = jnp.zeros((k, n_slots), F32)
    for c in range(PART):
        total = jnp.where(lane == c, wide[c * k : c * k + k], total)
    return total


def to_rows(columns):
    width = columns.shape[1] // PART
    tall = jnp.concatenate([columns[:, c * width : c * width + width] for c in range(PART)], 0)
    return tall.T.astype(BF)


def from_tall(tall):
    k = tall.shape[0] // PART
    return jnp.concatenate([tall[c * k : c * k + k] for c in range(PART)], 1)


def part_rows(n_rows, per_peer, parts):
    n_parts = n_rows // per_peer * parts
    rows = lax.broadcasted_iota(jnp.int32, (n_rows, 1), 0)
    part = lax.rem(rows, per_peer)
    source = jnp.where(part < parts, rows // per_peer * parts + part, -1)
    return hot(lax.broadcasted_iota(jnp.int32, (1, n_parts), 1) == source)


def slots_of(send_rows, send_counts, v_count):
    n_peers, cap = send_rows.shape
    n_slots = n_peers * cap
    parts = cap // PART
    width = n_peers * parts
    slots = lax.broadcasted_iota(jnp.int32, (1, n_slots), 1)
    within = lax.rem(slots, width)
    place = lax.rem(within, parts) * PART + slots // width
    chosen = hot(lax.broadcasted_iota(jnp.int32, (n_peers, 1), 0) == peer_at(within // parts, n_peers))
    base = 32
    high = send_rows // base
    low = send_rows - high * base
    both = matmul(high.astype(F32).astype(BF), chosen, 0, 0) * base + matmul(
        low.astype(F32).astype(BF), chosen, 0, 0
    )
    c = lax.broadcasted_iota(jnp.int32, (cap, n_slots), 0)
    rows = jnp.sum(jnp.where(c == place, both, 0.0), 0, keepdims=True)
    counts = jnp.broadcast_to(send_counts.astype(F32), (8, n_peers)).astype(BF)
    counts = matmul(counts, chosen)[:1]
    return jnp.where(place.astype(F32) >= counts, float(v_count), rows).astype(jnp.int32)


def pack_kernel(edges_ref, blocks_ref, copies_ref):
    n_tiles, _, width = edges_ref.shape
    sources, targets = edges_ref[:, 0, :], edges_ref[:, 1, :]
    packed = (targets << SHIFT) + (sources & ((1 << SHIFT) - 1))
    lane = lax.broadcasted_iota(jnp.int32, (n_tiles, width), 1)
    blocks = blocks_ref[...]
    blocks = jnp.where(lane == 0, blocks[:, :1], jnp.where(lane == 1, blocks[:, 1:2], 0))
    for r in range(copies_ref.shape[0]):
        copies_ref[r, :n_tiles, :] = packed
        copies_ref[r, n_tiles:, :] = blocks


def first_kernel(
    features_ref, send_rows_ref, send_counts_ref, replica_ref, table_ref, slots_ref, payload_ref
):
    k, v_count = table_ref.shape
    rows = lax.broadcasted_iota(jnp.int32, (k, features_ref.shape[1]), 0)
    columns = lax.broadcasted_iota(jnp.int32, (k, features_ref.shape[1]), 1)
    mine = hot(columns == rows + replica_ref[0] * k)
    table = matmul(mine, features_ref[...], 1, 1).astype(BF)
    table_ref[...] = table
    slots = slots_of(send_rows_ref[...], send_counts_ref[...], v_count)
    slots_ref[...] = slots
    payload_ref[...] = to_rows(pick(table, slots))


def inputs_kernel(
    features_ref, cotangent_ref, w_in_ref, b_in_ref, w_out_ref, b_out_ref, degree_ref, self_ref, gh_ref,
    vectors_ref,
):
    w_self = w_in_ref[: features_ref.shape[1], :].astype(F32).T.astype(BF)
    self_ref[...] = matmul(w_self, features_ref[...], 1, 1) + b_in_ref[...].T
    gh_ref[...] = matmul(w_out_ref[...], cotangent_ref[...], 1, 1)
    vectors_ref[...] = jnp.zeros_like(vectors_ref)
    vectors_ref[:1, :] = degree_ref[...].astype(F32)
    vectors_ref[1:2, : b_out_ref.shape[1]] = b_out_ref[...]


def edges_kernel(
    cap, per_peer, transpose, arrived_ref, owned_ref, edges_ref, blocks_ref, ready_ref, payload_ref,
    own_ref, table, total,
):
    del ready_ref
    k, v_count = owned_ref.shape
    own_blocks = v_count // LANES
    all_blocks = table.shape[0]
    arrived = arrived_ref[...]
    mirrors = from_peers(arrived, per_peer, cap)
    owned = owned_ref[...].astype(F32)
    for b in range(own_blocks):
        table[b] = owned[:, b * LANES : b * LANES + LANES]
    for b in range(own_blocks, all_blocks):
        first = (b - own_blocks) * LANES
        table[b] = mirrors[:, first : first + LANES]
    total[...] = jnp.zeros_like(total)
    n_groups, group_rows, width = edges_ref.shape
    per_group = group_rows // 2
    positions = lax.broadcasted_iota(jnp.int32, (LANES, width), 0)
    a, b = (1, 0) if transpose else (0, 1)
    together = math.gcd(n_groups, GROUPS)
    tiles = [(j, t) for j in range(together) for t in range(per_group)]

    def group(i, carry):
        g = i * together

        def slots(tile, side):
            packed = edges_ref[g + tile[0], tile[1] : tile[1] + 1, :]
            return packed >> SHIFT if side else packed & ((1 << SHIFT) - 1)

        def block(tile, side):
            return blocks_ref[g + tile[0], 2 * tile[1] + side]

        gathered = []
        for tile in tiles:
            lanes = jnp.broadcast_to(slots(tile, a) & (LANES - 1), (k, width))
            values = jnp.take_along_axis(table[block(tile, a)], lanes, axis=1, mode="promise_in_bounds")
            gathered.append(values.astype(BF))
        placed = []
        for n in range(0, len(tiles), 2):
            left = jnp.concatenate(gathered[n : n + 2], 0)
            right = jnp.concatenate([hot(positions == slots(tile, b)) for tile in tiles[n : n + 2]], 0)
            product = matmul(left, right, 1, 1)
            placed.extend([product[:k, :LANES], product[k:, LANES:]])
        for tile, values in zip(tiles, placed):
            at = block(tile, b)
            total[at] = total[at] + values
        return carry

    lax.fori_loop(0, n_groups // together, group, 0)
    for b in range(own_blocks):
        own_ref[:, b * LANES : b * LANES + LANES] = total[b]
    back = jnp.concatenate([total[b] for b in range(own_blocks, all_blocks)], 1)
    outgoing = to_peers(back, per_peer, cap)
    if per_peer > cap // PART:
        parts = per_peer - cap // PART
        rows = lax.broadcasted_iota(jnp.int32, (8, arrived.shape[0]), 1)
        part = lax.broadcasted_iota(jnp.int32, (8, arrived.shape[0]), 0)
        chosen = hot(lax.rem(rows, per_peer) == part + cap // PART)
        sums = matmul(chosen, arrived)
        place = lax.rem(lax.broadcasted_iota(jnp.int32, outgoing.shape, 0), per_peer)
        for h in range(parts):
            outgoing = jnp.where(place == cap // PART + h, sums[h : h + 1], outgoing)
    payload_ref[...] = outgoing.astype(BF)


def aggregate_kernel(arrived_ref, own_ref, slots_ref, vectors_ref, aggregate_ref, copies_ref):
    k, v_count = own_ref.shape
    returned = from_tall(arrived_ref[...].astype(F32).T.astype(BF))
    summed = own_ref[...] + scatter(returned, slots_ref[...], v_count)
    aggregate = (summed / vectors_ref[:1, :]).astype(BF)
    aggregate_ref[...] = aggregate
    for r in range(copies_ref.shape[0]):
        copies_ref[r] = aggregate


def dense_kernel(
    scale, cap, aggregate_ref, self_ref, gh_ref, w_in_ref, vectors_ref, slots_ref, table_ref, mine_ref,
    cotangent_ref, w_out_ref, replica_ref, output_ref, grad_self_ref, spread_ref, payload_ref,
    hidden_ref, grad_pre_ref, rows_ref,
):
    k, v_count = spread_ref.shape
    n_dp = aggregate_ref.shape[0]
    channels = n_dp * k
    aggregate = jnp.concatenate([aggregate_ref[place_of(r, n_dp)] for r in range(n_dp)], 0)
    pre = self_ref[...] + matmul(w_in_ref[channels:, :], aggregate, 0, 0)
    sigmoid = 1.0 / (1.0 + jnp.exp(-pre))
    hidden_ref[...] = (pre * sigmoid).astype(BF)
    grad_pre = (gh_ref[...] * (sigmoid * (1.0 + pre * (1.0 - sigmoid)))).astype(BF)
    grad_pre_ref[...] = grad_pre
    share = output_ref.shape[0]
    per_block = LANES // share
    block = pl.multiple_of((replica_ref[0] // per_block) * LANES, LANES)
    half = pl.multiple_of(lax.rem(replica_ref[0], per_block) * share, share)
    rows_ref[0] = matmul(hidden_ref[:, pl.ds(block, LANES)], w_out_ref[...], 0, 0)
    output_ref[...] = (rows_ref[0, pl.ds(half, share), :] + vectors_ref[1:2, :channels]).astype(BF)
    rows_ref[1] = matmul(w_in_ref[:channels, :], grad_pre_ref[:, pl.ds(block, LANES)]).T
    grad_self_ref[...] = rows_ref[1, pl.ds(half, share), :]
    first = pl.multiple_of(replica_ref[0] * k, k)
    spread = matmul(w_in_ref[pl.ds(pl.multiple_of(channels + first, k), k), :], grad_pre)
    spread = (spread / vectors_ref[:1, :]).astype(BF)
    spread_ref[...] = spread

    ones = jnp.ones((k, v_count), BF)
    left = jnp.concatenate([table_ref[...], mine_ref[...], ones], 0)
    grads_in = (matmul(left, grad_pre, 1, 1) * scale).astype(BF)
    left = jnp.concatenate([hidden_ref[pl.ds(first, k), :], ones], 0)
    grads_out = (matmul(left, cotangent_ref[...]) * scale).astype(BF)
    grads = jnp.concatenate([grads_in[: 2 * k], grads_out[:k], grads_in[2 * k :], grads_out[k:]], 0)

    parts = cap // PART
    halves = channels // LANES
    per_peer = parts + halves
    picked = to_rows(pick(spread, slots_ref[...]))
    n_rows = picked.shape[0] // parts * per_peer
    payload = matmul(part_rows(n_rows, per_peer, parts), picked)
    rows = lax.broadcasted_iota(jnp.int32, (n_rows, grads.shape[0]), 0)
    source = lax.broadcasted_iota(jnp.int32, (n_rows, grads.shape[0]), 1)
    peer = jnp.where(source == 4 * k, 3 * k + 1, jnp.where(source > 3 * k, -1, source))
    for h in range(halves):
        chosen = hot((peer_at(rows // per_peer, n_rows // per_peer) == peer) & (lax.rem(rows, per_peer) == parts + h))
        payload = payload + matmul(chosen, grads[:, h * LANES : h * LANES + LANES])
    payload_ref[...] = payload.astype(BF)


def back_kernel(cap, per_peer, arrived_ref, own_ref, slots_ref, copies_ref):
    k, v_count = own_ref.shape
    n_dp = copies_ref.shape[0]
    share = v_count // n_dp
    arrived = arrived_ref[...]
    tall = matmul(arrived, part_rows(arrived.shape[0], per_peer, cap // PART), 0, 0)
    returned = from_tall(tall.astype(BF))
    summed = (own_ref[...] + scatter(returned, slots_ref[...], v_count)).astype(BF)
    n_rows = copies_ref.shape[1] - k
    parts = cap // PART
    halves = per_peer - parts
    to = lax.broadcasted_iota(jnp.int32, (n_rows, arrived.shape[0]), 0)
    source = lax.broadcasted_iota(jnp.int32, (n_rows, arrived.shape[0]), 1)
    peer = peer_at(source // per_peer, arrived.shape[0] // per_peer)
    half = lax.rem(source, per_peer) - parts
    place = jnp.where(peer < 3 * k, half * (3 * k) + peer, halves * 3 * k + (peer - 3 * k) * halves + half)
    chosen = hot((place == to) & (half >= 0))
    grads = matmul(chosen, arrived).astype(BF)
    for r in range(n_dp):
        first = r * share // LANES * LANES
        copies_ref[place_of(r, n_dp), :k] = summed[:, first : first + LANES]
        copies_ref[place_of(r, n_dp), k:] = grads


def last_kernel(
    arrived_ref, grad_self_ref, rows_out_ref, replica_ref, output_ref, grad_features_ref, grad_w_in_ref,
    grad_b_in_ref, grad_w_out_ref, grad_b_out_ref, rows_ref,
):
    output_ref[...] = rows_out_ref[...]
    share, channels = grad_features_ref.shape
    n_dp = arrived_ref.shape[0]
    k = channels // n_dp
    half = pl.multiple_of(lax.rem(replica_ref[0], LANES // share) * share, share)
    columns = jnp.concatenate([arrived_ref[place_of(r, n_dp), :k] for r in range(n_dp)], 0)
    rows_ref[...] = columns.astype(F32).T
    grad_features_ref[...] = (rows_ref[pl.ds(half, share), :] + grad_self_ref[...]).astype(BF)
    halves = channels // LANES
    for h in range(halves):
        lanes = slice(h * LANES, h * LANES + LANES)
        first = k + h * 3 * k
        for r in range(n_dp):
            rows = slice(r * k, r * k + k)
            grad_w_in_ref[rows, lanes] = arrived_ref[place_of(r, n_dp), first : first + k].astype(F32)
            second = slice(channels + r * k, channels + r * k + k)
            grad_w_in_ref[second, lanes] = arrived_ref[place_of(r, n_dp), first + k : first + 2 * k].astype(F32)
            grad_w_out_ref[rows, lanes] = arrived_ref[place_of(r, n_dp), first + 2 * k : first + 3 * k].astype(F32)
        biases = arrived_ref[0, k + halves * 3 * k :].astype(F32)
        grad_b_in_ref[:, lanes] = biases[h : h + 1]
        grad_b_out_ref[:, lanes] = biases[halves + h : halves + h + 1]


def call(kernel, outs, args, smem=(), scratch=(), flops=0, name=None):
    in_specs = [
        pl.BlockSpec(memory_space=pltpu.SMEM if i in smem else pltpu.VMEM) for i in range(len(args))
    ]
    shapes = [jax.ShapeDtypeStruct(s, d) for s, d in outs]
    size = sum(math.prod(s) * jnp.dtype(d).itemsize for s, d in outs)
    size += sum(x.size * x.dtype.itemsize for x in args)
    return pl.pallas_call(
        kernel,
        out_shape=shapes,
        in_specs=in_specs,
        out_specs=[pl.BlockSpec(memory_space=pltpu.VMEM) for _ in outs],
        scratch_shapes=list(scratch),
        compiler_params=pltpu.CompilerParams(vmem_limit_bytes=8 * 1024 * 1024),
        cost_estimate=pl.CostEstimate(flops=flops, bytes_accessed=size, transcendentals=0),
        name=name,
    )(*args)


def swap(values, axis):
    size = lax.axis_size(axis)
    if axis == "dom":
        group = [peer_at(i, size) for i in range(size)]
    else:
        group = [replica_at(i, size) for i in range(size)]
    return lax.all_to_all(values, axis, split_axis=0, concat_axis=0, axis_index_groups=[group], tiled=True)


def on_device(
    features,
    degree,
    send_rows,
    send_counts,
    edge_slots,
    tile_blocks,
    w_in,
    b_in,
    w_out,
    b_out,
    cotangent,
):
    n_dp = lax.axis_size("dp")
    n_dom = lax.axis_size("dom")
    replica = lax.axis_index("dp").astype(jnp.int32).reshape(1)
    v_count, channels = features.shape
    cap = send_rows.shape[2]
    k = channels // n_dp
    share = v_count // n_dp
    n_slots = n_dom * cap
    n_tiles, _, tile_rows = edge_slots.shape[2:]
    blocks_count = (v_count + n_slots) // LANES
    scale = 1.0 / math.sqrt(v_count * n_dom)

    parts = cap // PART
    more = parts + channels // LANES

    (edges,) = call(
        pack_kernel,
        [((n_dp, 2 * n_tiles, tile_rows), jnp.int32)],
        [edge_slots[0, 0], tile_blocks[0, 0]],
        name="pack",
    )
    edges = swap(edges, "dp")
    blocks = edges[:, n_tiles:, :2].reshape(n_dp, 2 * n_tiles)

    table, slots_row, payload = call(
        first_kernel,
        [((k, v_count), BF), ((1, n_slots), jnp.int32), ((n_dom * parts, LANES), BF)],
        [features, send_rows[0], send_counts, replica],
        smem=(3,),
        name="first",
    )
    arrived = swap(payload, "dom")
    self_t, gh_t, vectors = call(
        inputs_kernel,
        [((channels, v_count), F32), ((channels, v_count), F32), ((8, v_count), F32)],
        [
            features, cotangent, w_in, b_in.reshape(1, -1), w_out, b_out.reshape(1, -1),
            degree.reshape(1, v_count),
        ],
        name="inputs",
    )

    def edge_pass(arrived, owned, per_peer, transpose):
        return call(
            lambda *refs: edges_kernel(cap, per_peer, transpose, *refs),
            [((n_dom * per_peer, LANES), BF), ((k, v_count), F32)],
            [arrived, owned, edges, blocks, vectors],
            smem=(3,),
            scratch=[
                pltpu.VMEM((blocks_count, k, LANES), F32),
                pltpu.VMEM((blocks_count, k, LANES), F32),
            ],
            name="edges_back" if transpose else "edges",
        )

    payload, own = edge_pass(arrived, table, parts, False)
    arrived = swap(payload, "dom")
    aggregate, copies = call(
        aggregate_kernel,
        [((k, v_count), BF), ((n_dp, k, v_count), BF)],
        [arrived, own, slots_row, vectors],
        name="aggregate",
    )
    aggregate_all = swap(copies, "dp")

    output, grad_self, spread, payload = call(
        lambda *refs: dense_kernel(scale, cap, *refs),
        [((share, channels), BF), ((share, channels), F32), ((k, v_count), BF), ((n_dom * more, LANES), BF)],
        [
            aggregate_all, self_t, gh_t, w_in, vectors, slots_row, table, aggregate, cotangent, w_out,
            replica,
        ],
        smem=(10,),
        scratch=[
            pltpu.VMEM((channels, v_count), BF),
            pltpu.VMEM((channels, v_count), BF),
            pltpu.VMEM((2, LANES, channels), F32),
        ],
        name="dense",
    )
    arrived = swap(payload, "dom")
    payload, own = edge_pass(arrived, spread, more, True)
    arrived = swap(payload, "dom")
    grad_rows = 2 * 3 * k + k
    (copies,) = call(
        lambda *refs: back_kernel(cap, more, *refs),
        [((n_dp, k + grad_rows, LANES), BF)],
        [arrived, own, slots_row],
        name="back",
    )
    arrived = swap(copies, "dp")
    output, grad_features, grad_w_in, grad_b_in, grad_w_out, grad_b_out = call(
        last_kernel,
        [
            ((share, channels), BF),
            ((share, channels), BF),
            ((2 * channels, channels), F32),
            ((1, channels), F32),
            ((channels, channels), F32),
            ((1, channels), F32),
        ],
        [arrived, grad_self, output, replica],
        smem=(3,),
        scratch=[pltpu.VMEM((LANES, channels), F32)],
        name="last",
    )
    return (output, grad_features, grad_w_in, grad_b_in[0], grad_w_out, grad_b_out[0])


def solution(mesh):
    in_specs = (
        P("dom", None),
        P("dom"),
        P("dom", None, None),
        P("dom", None),
        P("dom", "dp", None, None, None),
        P("dom", "dp", None, None),
        P(),
        P(),
        P(),
        P(),
        P("dom", None),
    )
    out_specs = (P(("dom", "dp"), None), P(("dom", "dp"), None), P(), P(), P(), P())
    return jax.shard_map(
        on_device, mesh=mesh, in_specs=in_specs, out_specs=out_specs, check_vma=False
    )
```
